256 devices in a mesh: row: 8 (over z_lo, y), col: 32 (over x, z_hi, core).
Axes of the slice: x: 4, y: 4, z: 8 (z_hi: 4, z_lo: 2; z = z_hi * 2 + z_lo), core: 2. Of those that a mesh axis runs over, the one named last changes fastest.
Arguments:
- inputs: bfloat16 [512, 8192], P('col', 'row'), may hold values from -6 to 6
- teacher: bfloat16 [512, 8192], P('col', 'row'), may hold values from -6 to 6
- gate_weight: bfloat16 [8192, 16384], P('row', 'col'), may hold values from -0.125 to 0.125
- up_weight: bfloat16 [8192, 16384], P('row', 'col'), may hold values from -0.125 to 0.125
- down_weight: bfloat16 [16384, 8192], P('col', 'row'), may hold values from -0.078125 to 0.078125
- block_mask: int32 [3, 64, 128], P(None, 'row', 'col'), may hold values 0 or 1
Outputs:
- student: bfloat16 [512, 8192], P('col', 'row')
- loss: float32 [], replicated
- grad_gate: bfloat16 [8192, 16384], P('row', 'col')
- grad_up: bfloat16 [8192, 16384], P('row', 'col')
- grad_down: bfloat16 [16384, 8192], P('col', 'row')
- grad_in: bfloat16 [512, 8192], P('col', 'row')
The draws below stay inside these ranges and needn't reach their ends.
All inputs are finite; a program needn't handle non-finite values. No bound on the sum of `block_mask` on one device may be relied on, other than what follows from the above.
Results may differ from the reference program's by a relative error of at most 0.0065.
Values may be sent and summed in bfloat16 or wider, within the bound.
No kernel may reach another device: no remote copies, remote signals or barrier semaphores. Data moves between devices by JAX's collectives and lax.ppermute only.
A program may use at most 64 MiB of HBM per device.

```python
import jax
import jax.numpy as jnp

D = 8192
FF = 16384
BLK = 128
TOKENS = 512


def touch_ends(result, stream_key, low, top_value):
    dims = result.shape
    spot = [jax.random.randint(jax.random.fold_in(stream_key, axis), (), 0, dims[axis]) for axis in range(len(dims))]
    result = result.at[tuple(spot)].set(low)
    longest = dims.index(max(dims))
    spot[longest] = (spot[longest] + 1) % dims[longest]
    return result.at[tuple(spot)].set(top_value)


def steps_of(rng, dims, shards, low, largest):
    def one(position, shards_of):
        heights = jax.random.uniform(jax.random.fold_in(jax.random.fold_in(rng, 6), position), (shards_of,), jnp.float32, low / len(shards), largest / len(shards))
        return jnp.repeat(jnp.exp(heights), dims[position] // shards_of).reshape((-1,) + (1,) * (len(dims) - position - 1))

    factor_of = one(*shards[0])
    for cut in shards[1:]:
        factor_of = factor_of * one(*cut)
    return factor_of


def centred(own_key, extent, scale, most, shards=(), dtype=jnp.bfloat16):
    loudness = steps_of(own_key, extent, shards, -0.22, 0.18) if shards else 1.0
    values = jax.random.normal(own_key, extent, jnp.float32) * scale * loudness
    return jnp.minimum(jnp.maximum(values, -most), most).astype(dtype)


def setup_inputs(seed: int = 0) -> dict:
    key_list = jax.random.split(jax.random.key(seed), 7)
    return {
        "inputs": centred(key_list[0], (TOKENS, D), 1.0, 6.0, ((0, 32), (1, 8))),
        "teacher": centred(key_list[1], (TOKENS, D), 1.0, 6.0, ((0, 32), (1, 8))),
        "gate_weight": centred(key_list[2], (D, FF), (3 * D // 10) ** -0.5, 0.125, ((0, 8), (1, 32))),
        "up_weight": centred(key_list[3], (D, FF), (3 * D // 10) ** -0.5, 0.125, ((0, 8), (1, 32))),
        "down_weight": centred(key_list[4], (FF, D), (3 * FF // 10) ** -0.5, 0.078125, ((0, 32), (1, 8))),
        "block_mask": touch_ends((jax.random.randint(key_list[5], (3, D // BLK, FF // BLK), 0, 10) < 3).astype(jnp.int32), jax.random.fold_in(key_list[5], 1), 0, 1),
    }


def spread(blocks):
    return jnp.repeat(jnp.repeat(blocks, BLK, axis=0), BLK, axis=1).astype(jnp.bfloat16)

def reference(inputs, teacher, gate_weight, up_weight, down_weight, block_mask):
    gate_keep = spread(block_mask[0])
    up_keep = spread(block_mask[1])
    down_keep = spread(block_mask[2]).T
    gate_kept = gate_weight * gate_keep
    up_kept = up_weight * up_keep
    down_kept = down_weight * down_keep
    gate = jnp.dot(inputs, gate_kept, preferred_element_type=jnp.float32)
    up = jnp.dot(inputs, up_kept, preferred_element_type=jnp.float32)
    sig = jax.nn.sigmoid(gate)
    act = gate * sig
    hidden = (act * up).astype(jnp.bfloat16)
    output = jnp.dot(hidden, down_kept, preferred_element_type=jnp.float32)
    diff = output - teacher.astype(jnp.float32)
    loss = jnp.sum(diff * diff) / (TOKENS * D)
    grad_out = (diff / jnp.sqrt(jnp.float32(TOKENS))).astype(jnp.bfloat16)
    grad_hidden = jnp.dot(grad_out, down_kept.T, preferred_element_type=jnp.float32)
    grad_down = jnp.dot(hidden.T, grad_out, preferred_element_type=jnp.float32)
    grad_down = (grad_down * down_keep).astype(jnp.bfloat16)
    grad_gate_act = (grad_hidden * up * sig * (1.0 + gate * (1.0 - sig))).astype(jnp.bfloat16)
    grad_up_act = (grad_hidden * act).astype(jnp.bfloat16)
    grad_gate = jnp.dot(inputs.T, grad_gate_act, preferred_element_type=jnp.float32)
    grad_gate = (grad_gate * gate_keep).astype(jnp.bfloat16)
    grad_up = jnp.dot(inputs.T, grad_up_act, preferred_element_type=jnp.float32)
    grad_up = (grad_up * up_keep).astype(jnp.bfloat16)
    grad_in = jnp.dot(grad_gate_act, gate_kept.T, preferred_element_type=jnp.float32)
    grad_in = grad_in + jnp.dot(grad_up_act, up_kept.T, preferred_element_type=jnp.float32)
    return (output.astype(jnp.bfloat16), loss, grad_gate, grad_up, grad_down, grad_in.astype(jnp.bfloat16))
```

```python
import functools

import jax
import jax.numpy as jnp
from jax import lax
from jax.experimental import pallas as pl
from jax.experimental.pallas import tpu as pltpu
from jax.sharding import PartitionSpec as P

D = 8192
BLK = 128
X, Z, CORES = 4, 4, 2
CHIPS = X * Z
ROWS = 8
TILE = 512
DOWN = 2
VMEM = pl.BlockSpec(memory_space=pltpu.VMEM)
SMEM = pl.BlockSpec(memory_space=pltpu.SMEM)
ANY = pl.BlockSpec(memory_space=pl.ANY)


def call(kernel, shapes, *args, flops=0, vmem=12, in_specs=None, after=(), beside=False, **kwargs):
    moved = sum(a.size * a.dtype.itemsize for a in args)
    moved += sum(s.size * s.dtype.itemsize for s in jax.tree.leaves(shapes))
    return pl.pallas_call(
        lambda *refs: kernel(*refs[: len(args)], *refs[len(args) + len(after) :]),
        out_shape=shapes,
        in_specs=(in_specs or [VMEM] * len(args)) + [ANY] * len(after),
        compiler_params=pltpu.CompilerParams(vmem_limit_bytes=vmem << 20),
        cost_estimate=pl.CostEstimate(
            flops=0 if beside else flops, bytes_accessed=0 if beside else moved, transcendentals=0
        ),
        **kwargs,
    )(*args, *after)


def shaped(shape, dtype=jnp.bfloat16):
    return jax.ShapeDtypeStruct(shape, dtype)


DONE = shaped((8, BLK), jnp.float32)


def join_kernel(*refs):
    joined_ref = refs[-1]
    size = refs[0].shape[0]
    for part, ref in enumerate(refs[:-1]):
        joined_ref[pl.ds(part * size, size), :] = ref[...]


def keep_kernel(mask_ref, gate_ref, up_ref, down_ref, *kept_refs):
    for which, (ref, kept_ref) in enumerate(zip((gate_ref, up_ref, down_ref), kept_refs)):
        for row in range(ref.shape[0] // BLK):
            for col in range(ref.shape[1] // BLK):
                at = (row, col) if which == DOWN else (col, row)
                keep = mask_ref[which, at[0], at[1]].astype(jnp.float32).astype(jnp.bfloat16)
                block = (pl.ds(row * BLK, BLK), pl.ds(col * BLK, BLK))
                kept_ref[block] = ref[block] * keep


def plain_dot(left, right):
    return jnp.dot(left, right, preferred_element_type=jnp.float32)


def other_turned_dot(left, right):
    return lax.dot_general(left, right, (((1,), (1,)), ((), ())), preferred_element_type=jnp.float32)


def gate_up_kernel(*refs):
    slabs, weights, (out_ref, rows_ref) = refs[:X], refs[X:-2], refs[-2:]
    join_kernel(*slabs, rows_ref)
    for which, ref in enumerate(weights):
        units = ref.shape[1]
        value = plain_dot(rows_ref[...], ref[...])
        out_ref[:, pl.ds(which * units, units)] = value.astype(out_ref.dtype)


def put_slabs(out_refs, cols, value):
    size = out_refs[0].shape[0]
    for part, ref in enumerate(out_refs):
        ref[:, cols] = value[part * size : (part + 1) * size].astype(ref.dtype)


def output_kernel(hidden_ref, down_ref, down_other_ref, *out_refs):
    units, width = down_ref.shape
    for at in range(0, width, TILE):
        cols = pl.ds(at, TILE)
        value = plain_dot(hidden_ref[:, :units], down_ref[:, cols])
        value = value + plain_dot(hidden_ref[:, units:], down_other_ref[:, cols])
        put_slabs(out_refs, cols, value)


def grad_hidden_kernel(*refs):
    slabs, (down_ref, down_other_ref, out_ref, grad_ref) = refs[:X], refs[X:]
    join_kernel(*slabs, grad_ref)
    units = down_ref.shape[0]
    squares = jnp.sum(jnp.square(grad_ref[...].astype(jnp.float32)), axis=0, keepdims=True)
    squares = jnp.sum(squares, axis=1, keepdims=True)
    lane = lax.broadcasted_iota(jnp.int32, (out_ref.shape[0], BLK), 1)
    terms = jnp.zeros(lane.shape, jnp.float32)
    for which in range(3):
        term = squares.astype(jnp.bfloat16).astype(jnp.float32)
        terms = jnp.where(lane == which, term, terms)
        squares = squares - term
    out_ref[:, pl.ds(2 * units, BLK)] = terms.astype(out_ref.dtype)
    for which, ref in enumerate((down_ref, down_other_ref)):
        value = other_turned_dot(grad_ref[...], ref[...])
        out_ref[:, pl.ds(which * units, units)] = value.astype(out_ref.dtype)


def grad_in_kernel(acts_ref, *refs):
    weights, out_refs = refs[:-X], refs[-X:]
    width, units = weights[0].shape
    for at in range(0, width, TILE):
        value = None
        for which, ref in enumerate(weights):
            term = other_turned_dot(acts_ref[:, pl.ds(which * units, units)], ref[pl.ds(at, TILE), :])
            value = term if value is None else value + term
        put_slabs(out_refs, pl.ds(at, TILE), value)


def multiply(kernel, shapes, left, weights, after=()):
    flops = 2 * sum(part.shape[0] for part in left) * sum(weight.size for weight in weights)
    return call(kernel, shapes, *left, *weights, flops=flops, vmem=16, after=after)


def summed(parts):
    total = parts[0][...].astype(jnp.float32)
    for part in parts[1:]:
        total = total + part[...].astype(jnp.float32)
    return total


def parts_of(parts_ref):
    return [parts_ref.at[part] for part in range(parts_ref.shape[0])]


def hidden_kernel(parts_ref, both_ref, copies_ref):
    both = summed(parts_of(parts_ref))
    half = both.shape[1] // 2
    gate, up = both[:, :half], both[:, half:]
    hidden = (gate * jax.nn.sigmoid(gate) * up).astype(jnp.bfloat16)
    both_ref[...] = both
    for part in range(copies_ref.shape[0]):
        copies_ref[part] = hidden


def error_kernel(scale, teacher_ref, *refs):
    parts, (student_ref, grad_ref) = refs[:-2], refs[-2:]
    output = summed(parts)
    student_ref[...] = output.astype(jnp.bfloat16)
    grad_ref[...] = ((output - teacher_ref[...].astype(jnp.float32)) / scale).astype(jnp.bfloat16)


def acts_kernel(parts_ref, both_ref, copies_ref, squares_ref):
    total = summed(parts_of(parts_ref))
    half = both_ref.shape[1] // 2
    grad_hidden = total[:, :half]
    squares_ref[...] = jnp.sum(total[:1, half:], axis=1, keepdims=True)
    gate, up = both_ref[:, :half], both_ref[:, half:]
    sig = jax.nn.sigmoid(gate)
    grad_gate_act = (grad_hidden * up * sig * (1.0 + gate * (1.0 - sig))).astype(jnp.bfloat16)
    grad_up_act = (grad_hidden * (gate * sig)).astype(jnp.bfloat16)
    for part in range(copies_ref.shape[0]):
        copies_ref[part, :, :half] = grad_gate_act
        copies_ref[part, :, half:] = grad_up_act


def sum_kernel(*refs):
    parts, out_refs = refs[:X], refs[X:]
    put_slabs(out_refs, slice(None), summed(parts))


def turned_dot(left, right):
    return lax.dot_general(left, right, (((0,), (0,)), ((), ())), preferred_element_type=jnp.float32)


def weights_kernel(which, mask_ref, rows_ref, rows_other_ref, acts_ref, acts_other_ref, out_ref, done_ref):
    width, units = out_ref.shape
    done_ref[...] = jnp.zeros_like(done_ref)
    for at in range(0, units, 2 * BLK):
        own = pl.ds(2 * which * units + at, 2 * BLK)
        other = pl.ds((2 * which + 1) * units + at, 2 * BLK)
        value = turned_dot(rows_ref[...], acts_ref[:, own])
        value = value + turned_dot(rows_other_ref[...], acts_other_ref[:, other])
        for row in range(width // BLK):
            for col in range(2):
                keep = mask_ref[which, at // BLK + col, row].astype(jnp.float32)
                block = value[row * BLK : (row + 1) * BLK, col * BLK : (col + 1) * BLK] * keep
                out_ref[pl.ds(row * BLK, BLK), pl.ds(at + col * BLK, BLK)] = block.astype(jnp.bfloat16)


def down_kernel(
    mask_ref,
    hidden_ref,
    hidden_other_ref,
    grad_ref,
    grad_other_ref,
    squares_ref,
    squares_other_ref,
    out_ref,
    loss_ref,
    done_ref,
):
    units, width = out_ref.shape
    loss_ref[...] = (squares_ref[...] + squares_other_ref[...]) * (1.0 / D)
    done_ref[...] = jnp.zeros_like(done_ref)
    for at in range(0, width, 2 * BLK):
        cols = pl.ds(at, 2 * BLK)
        value = turned_dot(hidden_ref[:, :units], grad_ref[:, cols])
        value = value + turned_dot(hidden_other_ref[:, units:], grad_other_ref[:, cols])
        for row in range(units // BLK):
            for col in range(2):
                keep = mask_ref[DOWN, row, at // BLK + col].astype(jnp.float32)
                block = value[row * BLK : (row + 1) * BLK, col * BLK : (col + 1) * BLK] * keep
                out_ref[pl.ds(row * BLK, BLK), pl.ds(at + col * BLK, BLK)] = block.astype(jnp.bfloat16)


def other_core(value):
    count = CHIPS * CORES
    return lax.ppermute(value, "col", [(device, device ^ 1) for device in range(count)])


def fetch(value, dx, dz):
    pairs = [
        ((((x + dx) % X * Z + (z + dz) % Z) * CORES + core), (x * Z + z) * CORES + core)
        for x in range(X)
        for z in range(Z)
        for core in range(CORES)
    ]
    return lax.ppermute(value, "col", pairs)


def gather_z(block):
    return [block] + [fetch(block, 0, step) for step in range(1, Z)]


def joined(parts):
    size, width = parts[0].shape
    return call(join_kernel, shaped((len(parts) * size, width)), *parts)


def gather_x(block):
    return [block] + [fetch(block, step, 0) for step in range(1, X)]


def spread_x(parts):
    return [parts[0]] + [fetch(parts[step], -step, 0) for step in range(1, X)]


def spread_z(parts):
    return [parts[0]] + [fetch(parts[step], 0, -step) for step in range(1, Z)]


def exchange_row(value):
    return lax.all_to_all(value, "row", 0, 0)


def flat(value):
    return value.reshape((-1,) + value.shape[2:])


def split(value, count):
    return value.reshape((count, -1) + value.shape[1:])


def per_device(inputs, teacher, gate_weight, up_weight, down_weight, block_mask):
    tokens, width = inputs.shape
    token_count = tokens * CHIPS * CORES
    units = gate_weight.shape[1]
    half = tokens * CHIPS
    scale = float(token_count) ** 0.5
    mask = jnp.transpose(block_mask, (0, 2, 1))
    slab = shaped((Z * tokens, width))
    piece = shaped((tokens, width))
    parts = gather_z(inputs)
    weights = call(
        keep_kernel,
        (shaped((width, units)),) * 2 + (shaped((units, width)),),
        mask,
        gate_weight,
        up_weight,
        down_weight,
        in_specs=[SMEM] + [VMEM] * 3,
        vmem=16,
        after=(parts[1],),
    )
    gates, ups, downs = ((value, other_core(value)) for value in weights)
    slabs = gather_x(joined(parts))
    partial, rows = multiply(
        gate_up_kernel, (shaped((half, 4 * units)), shaped((half, width))), slabs, gates + ups, downs[1:]
    )
    both, copies = call(
        hidden_kernel,
        (shaped((half // ROWS, 4 * units), jnp.float32), shaped((ROWS, half // ROWS, 2 * units))),
        exchange_row(split(partial, ROWS)),
    )
    hidden = flat(exchange_row(copies))
    slabs = spread_x(multiply(output_kernel, (slab,) * X, [hidden], downs))
    parts = spread_z(call(sum_kernel, (piece,) * Z, *slabs))
    student, grad_out = call(functools.partial(error_kernel, scale), (piece, piece), teacher, *parts)
    slabs = gather_x(joined(gather_z(grad_out)))
    partial, grad_rows = multiply(
        grad_hidden_kernel, (shaped((half, 2 * units + BLK)), shaped((half, width))), slabs, downs
    )
    copies, squares = call(
        acts_kernel,
        (shaped((ROWS, half // ROWS, 4 * units)), shaped((1, 1), jnp.float32)),
        exchange_row(split(partial, ROWS)),
        both,
    )
    acts = flat(exchange_row(copies))
    slabs = spread_x(multiply(grad_in_kernel, (slab,) * X, [acts], gates + ups))
    rows_other, hidden_other, grad_rows_other, acts_other, squares_other = (
        other_core(value) for value in (rows, hidden, grad_rows, acts, squares)
    )
    grad_down, loss, down_done = call(
        down_kernel,
        (shaped((units, width)), shaped((1, 1), jnp.float32), DONE),
        mask,
        hidden,
        hidden_other,
        grad_rows,
        grad_rows_other,
        squares,
        squares_other,
        in_specs=[SMEM] + [VMEM] * 6,
        flops=2 * token_count * width * units,
        vmem=16,
    )
    (grad_gate, gate_done), (grad_up, up_done) = (
        call(
            functools.partial(weights_kernel, which),
            (shaped((width, units)), DONE),
            mask,
            rows,
            rows_other,
            acts,
            acts_other,
            in_specs=[SMEM] + [VMEM] * 4,
            flops=2 * token_count * width * units,
            vmem=16,
        )
        for which in range(2)
    )
    parts = spread_z(call(sum_kernel, (piece,) * Z, *slabs, after=(down_done,)))
    (grad_in,) = call(sum_kernel, (piece,), *parts, after=(gate_done, up_done))
    return student, loss[0, 0], grad_gate, grad_up, grad_down, grad_in


def solution(mesh):
    return jax.shard_map(
        per_device,
        mesh=mesh,
        in_specs=(
            P("col", "row"),
            P("col", "row"),
            P("row", "col"),
            P("row", "col"),
            P("col", "row"),
            P(None, "row", "col"),
        ),
        out_specs=(
            P("col", "row"),
            P(),
            P("row", "col"),
            P("row", "col"),
            P("col", "row"),
            P("col", "row"),
        ),
        check_vma=False,
    )
```

```python
import functools

import jax
import jax.numpy as jnp
from jax import lax
from jax.experimental import pallas as pl
from jax.experimental.pallas import tpu as pltpu
from jax.sharding import PartitionSpec as P

D = 8192
BLK = 128
X, Z, CORES = 4, 4, 2
CHIPS = X * Z
ROWS = 8
TILE = 512
DOWN = 2
SAME_CORE = [[chip * CORES + core for chip in range(CHIPS)] for core in range(CORES)]
VMEM = pl.BlockSpec(memory_space=pltpu.VMEM)
SMEM = pl.BlockSpec(memory_space=pltpu.SMEM)
ANY = pl.BlockSpec(memory_space=pl.ANY)


def call(kernel, shapes, *args, flops=0, vmem=12, in_specs=None, after=(), beside=False, **kwargs):
    moved = sum(a.size * a.dtype.itemsize for a in args)
    moved += sum(s.size * s.dtype.itemsize for s in jax.tree.leaves(shapes))
    return pl.pallas_call(
        lambda *refs: kernel(*refs[: len(args)], *refs[len(args) + len(after) :]),
        out_shape=shapes,
        in_specs=(in_specs or [VMEM] * len(args)) + [ANY] * len(after),
        compiler_params=pltpu.CompilerParams(vmem_limit_bytes=vmem << 20),
        cost_estimate=pl.CostEstimate(
            flops=0 if beside else flops, bytes_accessed=0 if beside else moved, transcendentals=0
        ),
        **kwargs,
    )(*args, *after)


def shaped(shape, dtype=jnp.bfloat16):
    return jax.ShapeDtypeStruct(shape, dtype)


DONE = shaped((8, BLK), jnp.float32)


def join_kernel(*refs):
    joined_ref = refs[-1]
    size = refs[0].shape[0]
    for part, ref in enumerate(refs[:-1]):
        joined_ref[pl.ds(part * size, size), :] = ref[...]


def copies_kernel(block_ref, copies_ref):
    for part in range(copies_ref.shape[0]):
        copies_ref[part] = block_ref[...]


def turn_kernel(ref, turned_ref):
    turned_ref[...] = ref[...].T


def keep(mask_ref, which, ref, kept_ref):
    for row in range(ref.shape[0] // BLK):
        for col in range(ref.shape[1] // BLK):
            at = (row, col) if which == DOWN else (col, row)
            factor = mask_ref[which, at[0], at[1]].astype(jnp.float32).astype(jnp.bfloat16)
            block = (pl.ds(row * BLK, BLK), pl.ds(col * BLK, BLK))
            kept_ref[block] = ref[block] * factor


def plain_dot(left, right):
    return jnp.dot(left, right, preferred_element_type=jnp.float32)


def other_turned_dot(left, right):
    return lax.dot_general(left, right, (((1,), (1,)), ((), ())), preferred_element_type=jnp.float32)


def gate_up_kernel(mask_ref, mask_other_ref, chips_ref, *refs):
    weights, kept_refs, (out_ref, rows_ref) = refs[:4], refs[4:8], refs[8:]
    chip = lax.axis_index("col") // CORES
    size = chips_ref.shape[1]
    for part in range(CHIPS):
        x = lax.rem(chip // Z + part // Z, X)
        z = lax.rem(chip + part % Z, Z)
        rows_ref[pl.ds(part * size, size), :] = chips_ref[x * Z + z]
    for which, (ref, kept_ref) in enumerate(zip(weights, kept_refs)):
        units = ref.shape[1]
        keep((mask_ref, mask_other_ref)[which % 2], which // 2, ref, kept_ref)
        value = plain_dot(rows_ref[...], kept_ref[...])
        out_ref[:, pl.ds(which * units, units)] = value.astype(out_ref.dtype)


def put_slabs(out_refs, cols, value):
    size = out_refs[0].shape[0]
    for part, ref in enumerate(out_refs):
        ref[:, cols] = value[part * size : (part + 1) * size].astype(ref.dtype)


def output_kernel(mask_ref, mask_other_ref, hidden_ref, down_ref, down_other_ref, kept_ref, kept_other_ref, *out_refs):
    units, width = down_ref.shape
    keep(mask_ref, DOWN, down_ref, kept_ref)
    keep(mask_other_ref, DOWN, down_other_ref, kept_other_ref)
    for at in range(0, width, TILE):
        cols = pl.ds(at, TILE)
        value = plain_dot(hidden_ref[:, :units], kept_ref[:, cols])
        value = value + plain_dot(hidden_ref[:, units:], kept_other_ref[:, cols])
        put_slabs(out_refs, cols, value)


def grad_hidden_kernel(*refs):
    slabs, (down_ref, down_other_ref, out_ref, grad_ref) = refs[:X], refs[X:]
    join_kernel(*slabs, grad_ref)
    units = down_ref.shape[0]
    squares = jnp.sum(jnp.square(grad_ref[...].astype(jnp.float32)), axis=0, keepdims=True)
    squares = jnp.sum(squares, axis=1, keepdims=True)
    lane = lax.broadcasted_iota(jnp.int32, (out_ref.shape[0], BLK), 1)
    terms = jnp.zeros(lane.shape, jnp.float32)
    for which in range(3):
        term = squares.astype(jnp.bfloat16).astype(jnp.float32)
        terms = jnp.where(lane == which, term, terms)
        squares = squares - term
    out_ref[:, pl.ds(2 * units, BLK)] = terms.astype(out_ref.dtype)
    for which, ref in enumerate((down_ref, down_other_ref)):
        value = other_turned_dot(grad_ref[...], ref[...])
        out_ref[:, pl.ds(which * units, units)] = value.astype(out_ref.dtype)


def grad_in_kernel(acts_ref, *refs):
    weights, out_refs = refs[:-X], refs[-X:]
    width, units = weights[0].shape
    for at in range(0, width, TILE):
        value = None
        for which, ref in enumerate(weights):
            term = other_turned_dot(acts_ref[:, pl.ds(which * units, units)], ref[pl.ds(at, TILE), :])
            value = term if value is None else value + term
        put_slabs(out_refs, pl.ds(at, TILE), value)


def multiply(kernel, shapes, left, weights, masks=(), after=()):
    flops = 2 * sum(part.size // part.shape[-1] for part in left) * sum(weight.size for weight in weights)
    specs = [SMEM] * len(masks) + [VMEM] * (len(left) + len(weights))
    return call(kernel, shapes, *masks, *left, *weights, flops=flops, vmem=16, in_specs=specs, after=after)


def summed(parts):
    total = parts[0][...].astype(jnp.float32)
    for part in parts[1:]:
        total = total + part[...].astype(jnp.float32)
    return total


def parts_of(parts_ref):
    return [parts_ref.at[part] for part in range(parts_ref.shape[0])]


def hidden_kernel(parts_ref, both_ref, copies_ref):
    both = summed(parts_of(parts_ref))
    half = both.shape[1] // 2
    gate, up = both[:, :half], both[:, half:]
    hidden = (gate * jax.nn.sigmoid(gate) * up).astype(jnp.bfloat16)
    both_ref[...] = both
    for part in range(copies_ref.shape[0]):
        copies_ref[part] = hidden


def lessen_kernel(teacher_ref, *refs):
    parts, (own_ref, slab_ref) = refs[:X], refs[X:]
    size = own_ref.shape[0]
    total = summed(parts)
    own_ref[...] = total[:size]
    slab_ref[pl.ds(0, size), :] = (total[:size] - teacher_ref[...].astype(jnp.float32)).astype(jnp.bfloat16)
    slab_ref[pl.ds(size, (Z - 1) * size), :] = total[size:].astype(jnp.bfloat16)


def error_kernel(scale, own_ref, *refs):
    slabs, (student_ref, grad_ref) = refs[:Z], refs[Z:]
    size = own_ref.shape[0]
    for part in range(Z):
        terms = [
            slabs[step][pl.ds((part - step) % Z * size, size), :].astype(jnp.float32) for step in range(Z)
        ]
        diff = (terms[0] + terms[2]) + (terms[1] + terms[3])
        grad_ref[pl.ds(part * size, size), :] = (diff / scale).astype(jnp.bfloat16)
        if part == 0:
            student_ref[...] = (own_ref[...] + terms[2] + terms[1] + terms[3]).astype(jnp.bfloat16)


def acts_kernel(parts_ref, both_ref, copies_ref, squares_ref):
    total = summed(parts_of(parts_ref))
    half = both_ref.shape[1] // 2
    grad_hidden = total[:, :half]
    squares_ref[...] = jnp.sum(total[:1, half:], axis=1, keepdims=True)
    gate, up = both_ref[:, :half], both_ref[:, half:]
    sig = jax.nn.sigmoid(gate)
    grad_gate_act = (grad_hidden * up * sig * (1.0 + gate * (1.0 - sig))).astype(jnp.bfloat16)
    grad_up_act = (grad_hidden * (gate * sig)).astype(jnp.bfloat16)
    for part in range(copies_ref.shape[0]):
        copies_ref[part, :, :half] = grad_gate_act
        copies_ref[part, :, half:] = grad_up_act


def sum_kernel(*refs):
    parts, out_refs = refs[:X], refs[X:]
    put_slabs(out_refs, slice(None), summed(parts))


def weights_kernel(which, mask_ref, rows_ref, rows_other_ref, acts_ref, acts_other_ref, out_ref, done_ref):
    width, units = out_ref.shape
    done_ref[...] = jnp.zeros_like(done_ref)
    for at in range(0, units, 2 * BLK):
        own = pl.ds(2 * which * units + at, 2 * BLK)
        other = pl.ds((2 * which + 1) * units + at, 2 * BLK)
        value = plain_dot(rows_ref[...], acts_ref[:, own])
        value = value + plain_dot(rows_other_ref[...], acts_other_ref[:, other])
        for row in range(width // BLK):
            for col in range(2):
                keep = mask_ref[which, at // BLK + col, row].astype(jnp.float32)
                block = value[row * BLK : (row + 1) * BLK, col * BLK : (col + 1) * BLK] * keep
                out_ref[pl.ds(row * BLK, BLK), pl.ds(at + col * BLK, BLK)] = block.astype(jnp.bfloat16)


def down_kernel(
    mask_ref,
    hidden_ref,
    hidden_other_ref,
    grad_ref,
    grad_other_ref,
    squares_ref,
    squares_other_ref,
    out_ref,
    loss_ref,
    done_ref,
):
    units, width = out_ref.shape
    loss_ref[...] = (squares_ref[...] + squares_other_ref[...]) * (1.0 / D)
    done_ref[...] = jnp.zeros_like(done_ref)
    for at in range(0, width, 2 * BLK):
        cols = pl.ds(at, 2 * BLK)
        value = plain_dot(hidden_ref[pl.ds(0, units), :], grad_ref[:, cols])
        value = value + plain_dot(hidden_other_ref[pl.ds(units, units), :], grad_other_ref[:, cols])
        for row in range(units // BLK):
            for col in range(2):
                keep = mask_ref[DOWN, row, at // BLK + col].astype(jnp.float32)
                block = value[row * BLK : (row + 1) * BLK, col * BLK : (col + 1) * BLK] * keep
                out_ref[pl.ds(row * BLK, BLK), pl.ds(at + col * BLK, BLK)] = block.astype(jnp.bfloat16)


def other_core(value):
    count = CHIPS * CORES
    return lax.ppermute(value, "col", [(device, device ^ 1) for device in range(count)])


def fetch(value, dx, dz):
    pairs = [
        ((((x + dx) % X * Z + (z + dz) % Z) * CORES + core), (x * Z + z) * CORES + core)
        for x in range(X)
        for z in range(Z)
        for core in range(CORES)
    ]
    return lax.ppermute(value, "col", pairs)


def gather_z(block):
    return [block] + [fetch(block, 0, step) for step in range(1, Z)]


def gather_x(block):
    return [block] + [fetch(block, step, 0) for step in range(1, X)]


def spread_x(parts):
    return [parts[0]] + [fetch(parts[step], -step, 0) for step in range(1, X)]


def spread_z(parts):
    return [parts[0]] + [fetch(parts[step], 0, -step) for step in range(1, Z)]


def exchange_row(value):
    return lax.all_to_all(value, "row", 0, 0)


def flat(value):
    return value.reshape((-1,) + value.shape[2:])


def split(value, count):
    return value.reshape((count, -1) + value.shape[1:])


def per_device(inputs, teacher, gate_weight, up_weight, down_weight, block_mask):
    tokens, width = inputs.shape
    token_count = tokens * CHIPS * CORES
    units = gate_weight.shape[1]
    half = tokens * CHIPS
    scale = float(token_count) ** 0.5
    mask = jnp.transpose(block_mask, (0, 2, 1))
    slab = shaped((Z * tokens, width))
    piece = shaped((tokens, width))
    wide, tall = shaped((width, units)), shaped((units, width))
    gates, ups, downs, masks = (
        (value, other_core(value)) for value in (gate_weight, up_weight, down_weight, mask)
    )
    copies = call(copies_kernel, shaped((CHIPS, tokens, width)), inputs, after=masks[1:])
    chips = lax.all_to_all(copies, "col", 0, 0, axis_index_groups=SAME_CORE)
    *gate_ups, partial, rows = multiply(
        gate_up_kernel,
        (wide,) * 4 + (shaped((half, 4 * units)), shaped((half, width))),
        [chips],
        gates + ups,
        masks,
        downs[1:],
    )
    both, copies = call(
        hidden_kernel,
        (shaped((half // ROWS, 4 * units), jnp.float32), shaped((ROWS, half // ROWS, 2 * units))),
        exchange_row(split(partial, ROWS)),
    )
    hidden = flat(exchange_row(copies))
    *downs, first, second, third, fourth = multiply(
        output_kernel, (tall,) * 2 + (slab,) * X, [hidden], downs, masks
    )
    slabs = spread_x([first, second, third, fourth])
    own, lessened = call(lessen_kernel, (shaped((tokens, width), jnp.float32), slab), teacher, *slabs)
    slabs = gather_z(lessened)
    rows_turned, hidden_turned = (
        call(turn_kernel, shaped(value.shape[::-1]), value, after=slabs[3:]) for value in (rows, hidden)
    )
    turned_other = [other_core(value) for value in (rows_turned, hidden_turned)]
    student, grad_out = call(functools.partial(error_kernel, scale), (piece, slab), own, *slabs)
    partial, grad_rows = multiply(
        grad_hidden_kernel,
        (shaped((half, 2 * units + BLK)), shaped((half, width))),
        gather_x(grad_out),
        downs,
        after=turned_other,
    )
    copies, squares = call(
        acts_kernel,
        (shaped((ROWS, half // ROWS, 4 * units)), shaped((1, 1), jnp.float32)),
        exchange_row(split(partial, ROWS)),
        both,
    )
    acts = flat(exchange_row(copies))
    slabs = spread_x(multiply(grad_in_kernel, (slab,) * X, [acts], gate_ups))
    grad_rows_other, acts_other, squares_other = (
        other_core(value) for value in (grad_rows, acts, squares)
    )
    grad_down, loss, down_done = call(
        down_kernel,
        (shaped((units, width)), shaped((1, 1), jnp.float32), DONE),
        mask,
        hidden_turned,
        turned_other[1],
        grad_rows,
        grad_rows_other,
        squares,
        squares_other,
        in_specs=[SMEM] + [VMEM] * 6,
        flops=2 * token_count * width * units,
        vmem=16,
    )
    (grad_gate, gate_done), (grad_up, up_done) = (
        call(
            functools.partial(weights_kernel, which),
            (shaped((width, units)), DONE),
            mask,
            rows_turned,
            turned_other[0],
            acts,
            acts_other,
            in_specs=[SMEM] + [VMEM] * 4,
            flops=2 * token_count * width * units,
            vmem=16,
        )
        for which in range(2)
    )
    parts = spread_z(call(sum_kernel, (piece,) * Z, *slabs, after=(down_done,)))
    (grad_in,) = call(sum_kernel, (piece,), *parts, after=(gate_done, up_done))
    return student, loss[0, 0], grad_gate, grad_up, grad_down, grad_in


def solution(mesh):
    return jax.shard_map(
        per_device,
        mesh=mesh,
        in_specs=(
            P("col", "row"),
            P("col", "row"),
            P("row", "col"),
            P("row", "col"),
            P("col", "row"),
            P(None, "row", "col"),
        ),
        out_specs=(
            P("col", "row"),
            P(),
            P("row", "col"),
            P("row", "col"),
            P("col", "row"),
            P("col", "row"),
        ),
        check_vma=False,
    )
```

```python
import functools

import jax
import jax.numpy as jnp
from jax import lax
from jax.experimental import pallas as pl
from jax.experimental.pallas import tpu as pltpu
from jax.sharding import PartitionSpec as P

D = 8192
BLK = 128
X, Z, CORES = 4, 4, 2
CHIPS = X * Z
ROWS = 8
TILE = 512
DOWN = 2
SAME_CORE = [[chip * CORES + core for chip in range(CHIPS)] for core in range(CORES)]
VMEM = pl.BlockSpec(memory_space=pltpu.VMEM)
SMEM = pl.BlockSpec(memory_space=pltpu.SMEM)
ANY = pl.BlockSpec(memory_space=pl.ANY)


def call(kernel, shapes, *args, flops=0, vmem=12, in_specs=None, after=(), beside=False, **kwargs):
    moved = sum(a.size * a.dtype.itemsize for a in args)
    moved += sum(s.size * s.dtype.itemsize for s in jax.tree.leaves(shapes))
    return pl.pallas_call(
        lambda *refs: kernel(*refs[: len(args)], *refs[len(args) + len(after) :]),
        out_shape=shapes,
        in_specs=(in_specs or [VMEM] * len(args)) + [ANY] * len(after),
        compiler_params=pltpu.CompilerParams(vmem_limit_bytes=vmem << 20),
        cost_estimate=pl.CostEstimate(
            flops=0 if beside else flops, bytes_accessed=0 if beside else moved, transcendentals=0
        ),
        **kwargs,
    )(*args, *after)


def shaped(shape, dtype=jnp.bfloat16):
    return jax.ShapeDtypeStruct(shape, dtype)


DONE = shaped((8, BLK), jnp.float32)


def join_kernel(*refs):
    joined_ref = refs[-1]
    size = refs[0].shape[0]
    for part, ref in enumerate(refs[:-1]):
        joined_ref[pl.ds(part * size, size), :] = ref[...]


def keep(mask_ref, which, ref, kept_ref):
    for row in range(ref.shape[0] // BLK):
        for col in range(ref.shape[1] // BLK):
            at = (row, col) if which == DOWN else (col, row)
            factor = mask_ref[which, at[0], at[1]].astype(jnp.float32).astype(jnp.bfloat16)
            block = (pl.ds(row * BLK, BLK), pl.ds(col * BLK, BLK))
            kept_ref[block] = ref[block] * factor


def plain_dot(left, right):
    return jnp.dot(left, right, preferred_element_type=jnp.float32)


def other_turned_dot(left, right):
    return lax.dot_general(left, right, (((1,), (1,)), ((), ())), preferred_element_type=jnp.float32)


def gate_up_kernel(mask_ref, mask_other_ref, chips_ref, *refs):
    weights, kept_refs, (out_ref, rows_ref) = refs[:4], refs[4:8], refs[8:]
    chip = lax.axis_index("col") // CORES
    size = chips_ref.shape[1]
    for part in range(CHIPS):
        x = lax.rem(chip // Z + part // Z, X)
        z = lax.rem(chip + part % Z, Z)
        rows_ref[pl.ds(part * size, size), :] = chips_ref[x * Z + z]
    for which, (ref, kept_ref) in enumerate(zip(weights, kept_refs)):
        units = ref.shape[1]
        keep((mask_ref, mask_other_ref)[which % 2], which // 2, ref, kept_ref)
        value = plain_dot(rows_ref[...], kept_ref[...])
        out_ref[:, pl.ds(which * units, units)] = value.astype(out_ref.dtype)


def put_slabs(out_refs, cols, value):
    size = out_refs[0].shape[0]
    for part, ref in enumerate(out_refs):
        ref[:, cols] = value[part * size : (part + 1) * size].astype(ref.dtype)


def output_kernel(mask_ref, mask_other_ref, hidden_ref, down_ref, down_other_ref, kept_ref, kept_other_ref, *out_refs):
    units, width = down_ref.shape
    keep(mask_ref, DOWN, down_ref, kept_ref)
    keep(mask_other_ref, DOWN, down_other_ref, kept_other_ref)
    for at in range(0, width, TILE):
        cols = pl.ds(at, TILE)
        value = plain_dot(hidden_ref[:, :units], kept_ref[:, cols])
        value = value + plain_dot(hidden_ref[:, units:], kept_other_ref[:, cols])
        put_slabs(out_refs, cols, value)


def grad_hidden_kernel(*refs):
    slabs, (down_ref, down_other_ref, out_ref, grad_ref) = refs[:X], refs[X:]
    join_kernel(*slabs, grad_ref)
    units = down_ref.shape[0]
    squares = jnp.sum(jnp.square(grad_ref[...].astype(jnp.float32)), axis=0, keepdims=True)
    squares = jnp.sum(squares, axis=1, keepdims=True)
    lane = lax.broadcasted_iota(jnp.int32, (out_ref.shape[0], BLK), 1)
    terms = jnp.zeros(lane.shape, jnp.float32)
    for which in range(3):
        term = squares.astype(jnp.bfloat16).astype(jnp.float32)
        terms = jnp.where(lane == which, term, terms)
        squares = squares - term
    out_ref[:, pl.ds(2 * units, BLK)] = terms.astype(out_ref.dtype)
    for which, ref in enumerate((down_ref, down_other_ref)):
        value = other_turned_dot(grad_ref[...], ref[...])
        out_ref[:, pl.ds(which * units, units)] = value.astype(out_ref.dtype)


def grad_in_kernel(acts_ref, *refs):
    weights, out_refs = refs[:-X], refs[-X:]
    width, units = weights[0].shape
    for at in range(0, width, TILE):
        value = None
        for which, ref in enumerate(weights):
            term = other_turned_dot(acts_ref[:, pl.ds(which * units, units)], ref[pl.ds(at, TILE), :])
            value = term if value is None else value + term
        put_slabs(out_refs, pl.ds(at, TILE), value)


def multiply(kernel, shapes, left, weights, masks=(), after=()):
    flops = 2 * sum(part.size // part.shape[-1] for part in left) * sum(weight.size for weight in weights)
    specs = [SMEM] * len(masks) + [VMEM] * (len(left) + len(weights))
    return call(kernel, shapes, *masks, *left, *weights, flops=flops, vmem=16, in_specs=specs, after=after)


def summed(parts):
    total = parts[0][...].astype(jnp.float32)
    for part in parts[1:]:
        total = total + part[...].astype(jnp.float32)
    return total


def parts_of(parts_ref):
    return [parts_ref.at[part] for part in range(parts_ref.shape[0])]


def hidden_kernel(parts_ref, both_ref, copies_ref):
    both = summed(parts_of(parts_ref))
    half = both.shape[1] // 2
    gate, up = both[:, :half], both[:, half:]
    hidden = (gate * jax.nn.sigmoid(gate) * up).astype(jnp.bfloat16)
    both_ref[...] = both
    for part in range(copies_ref.shape[0]):
        copies_ref[part] = hidden


def error_kernel(scale, teacher_ref, *refs):
    parts, (student_ref, grad_ref) = refs[:-2], refs[-2:]
    output = summed(parts)
    student_ref[...] = output.astype(jnp.bfloat16)
    grad_ref[...] = ((output - teacher_ref[...].astype(jnp.float32)) / scale).astype(jnp.bfloat16)


def acts_kernel(parts_ref, both_ref, copies_ref, squares_ref):
    total = summed(parts_of(parts_ref))
    half = both_ref.shape[1] // 2
    grad_hidden = total[:, :half]
    squares_ref[...] = jnp.broadcast_to(jnp.sum(total[:1, half:], axis=1, keepdims=True), squares_ref.shape)
    gate, up = both_ref[:, :half], both_ref[:, half:]
    sig = jax.nn.sigmoid(gate)
    grad_gate_act = (grad_hidden * up * sig * (1.0 + gate * (1.0 - sig))).astype(jnp.bfloat16)
    grad_up_act = (grad_hidden * (gate * sig)).astype(jnp.bfloat16)
    for part in range(copies_ref.shape[0]):
        copies_ref[part, :, :half] = grad_gate_act
        copies_ref[part, :, half:] = grad_up_act


def sum_kernel(*refs):
    parts, out_refs = refs[:X], refs[X:]
    put_slabs(out_refs, slice(None), summed(parts))


def put_kept(mask_ref, which, value, col, scratch_ref):
    for row in range(value.shape[0] // BLK):
        for step in range(value.shape[1] // BLK):
            at = (row, col + step) if which == DOWN else (col + step, row)
            factor = mask_ref[which, at[0], at[1]].astype(jnp.float32)
            block = value[row * BLK : (row + 1) * BLK, step * BLK : (step + 1) * BLK] * factor
            scratch_ref[pl.ds(row * BLK, BLK), pl.ds((col + step) * BLK, BLK)] = block.astype(jnp.bfloat16)


def weights_kernel(
    mask_ref,
    rows_ref,
    rows_other_ref,
    acts_ref,
    acts_other_ref,
    hidden_ref,
    hidden_other_ref,
    grad_ref,
    grad_other_ref,
    squares_ref,
    squares_other_ref,
    gate_ref,
    up_ref,
    down_ref,
    loss_ref,
    done_ref,
    gate_scratch,
    up_scratch,
    down_scratch,
    sems,
):
    units = gate_ref.shape[1]
    loss_ref[...] = (squares_ref[:1, :1] + squares_other_ref[:1, :1]) * (1.0 / D)
    done_ref[...] = jnp.zeros_like(done_ref)
    copies = []

    def put(which, value, col, scratch, out_ref):
        put_kept(mask_ref, which, value, col, scratch)
        cols = pl.ds(col * BLK, value.shape[1])
        copy = pltpu.make_async_copy(scratch.at[:, cols], out_ref.at[:, cols], sems.at[len(copies)])
        copy.start()
        copies.append(copy)

    turned, turned_other = hidden_ref[:, :units].T, hidden_other_ref[:, units:].T
    for col in range(0, down_ref.shape[1] // BLK, 4):
        cols = pl.ds(col * BLK, 4 * BLK)
        value = plain_dot(turned, grad_ref[:, cols]) + plain_dot(turned_other, grad_other_ref[:, cols])
        put(DOWN, value, col, down_scratch, down_ref)
    turned, turned_other = rows_ref[...].T, rows_other_ref[...].T
    for which, (scratch, out_ref) in enumerate(((gate_scratch, gate_ref), (up_scratch, up_ref))):
        for col in range(0, units // BLK, 2):
            own = pl.ds(2 * which * units + col * BLK, 2 * BLK)
            other = pl.ds((2 * which + 1) * units + col * BLK, 2 * BLK)
            value = plain_dot(turned, acts_ref[:, own]) + plain_dot(turned_other, acts_other_ref[:, other])
            put(which, value, col, scratch, out_ref)
    for copy in copies:
        copy.wait()


def other_core(value):
    count = CHIPS * CORES
    return lax.ppermute(value, "col", [(device, device ^ 1) for device in range(count)])


def fetch(value, dx, dz):
    pairs = [
        ((((x + dx) % X * Z + (z + dz) % Z) * CORES + core), (x * Z + z) * CORES + core)
        for x in range(X)
        for z in range(Z)
        for core in range(CORES)
    ]
    return lax.ppermute(value, "col", pairs)


def gather_z(block):
    return [block] + [fetch(block, 0, step) for step in range(1, Z)]


def joined(parts):
    size, width = parts[0].shape
    return call(join_kernel, shaped((len(parts) * size, width)), *parts)


def gather_x(block):
    return [block] + [fetch(block, step, 0) for step in range(1, X)]


def spread_x(parts):
    return [parts[0]] + [fetch(parts[step], -step, 0) for step in range(1, X)]


def spread_z(parts):
    return [parts[0]] + [fetch(parts[step], 0, -step) for step in range(1, Z)]


def exchange_row(value):
    return lax.all_to_all(value, "row", 0, 0)


def flat(value):
    return value.reshape((-1,) + value.shape[2:])


def split(value, count):
    return value.reshape((count, -1) + value.shape[1:])


def per_device(inputs, teacher, gate_weight, up_weight, down_weight, block_mask):
    tokens, width = inputs.shape
    token_count = tokens * CHIPS * CORES
    units = gate_weight.shape[1]
    half = tokens * CHIPS
    scale = float(token_count) ** 0.5
    mask = jnp.transpose(block_mask, (0, 2, 1))
    slab = shaped((Z * tokens, width))
    piece = shaped((tokens, width))
    wide, tall = shaped((width, units)), shaped((units, width))
    gates, ups, downs, masks = (
        (value, other_core(value)) for value in (gate_weight, up_weight, down_weight, mask)
    )
    copies = jnp.broadcast_to(inputs[None], (CHIPS, tokens, width))
    chips = lax.all_to_all(copies, "col", 0, 0, axis_index_groups=SAME_CORE)
    *gate_ups, partial, rows = multiply(
        gate_up_kernel,
        (wide,) * 4 + (shaped((half, 4 * units)), shaped((half, width))),
        [chips],
        gates + ups,
        masks,
        downs[1:],
    )
    both, copies = call(
        hidden_kernel,
        (shaped((half // ROWS, 4 * units), jnp.float32), shaped((ROWS, half // ROWS, 2 * units))),
        exchange_row(split(partial, ROWS)),
    )
    hidden = flat(exchange_row(copies))
    *downs, first, second, third, fourth = multiply(
        output_kernel, (tall,) * 2 + (slab,) * X, [hidden], downs, masks
    )
    slabs = spread_x([first, second, third, fourth])
    parts = spread_z(call(sum_kernel, (piece,) * Z, *slabs))
    student, grad_out = call(functools.partial(error_kernel, scale), (piece, piece), teacher, *parts)
    slabs = gather_x(joined(gather_z(grad_out)))
    partial, grad_rows = multiply(
        grad_hidden_kernel, (shaped((half, 2 * units + BLK)), shaped((half, width))), slabs, downs
    )
    copies, squares = call(
        acts_kernel,
        (shaped((ROWS, half // ROWS, 4 * units)), DONE),
        exchange_row(split(partial, ROWS)),
        both,
    )
    acts = flat(exchange_row(copies))
    slabs = spread_x(multiply(grad_in_kernel, (slab,) * X, [acts], gate_ups))
    rows_other, hidden_other, grad_rows_other, acts_other, squares_other = (
        other_core(value) for value in (rows, hidden, grad_rows, acts, squares)
    )
    grad_gate, grad_up, grad_down, loss, done = call(
        weights_kernel,
        (wide, wide, tall, shaped((1, 1), jnp.float32), DONE),
        mask,
        rows,
        rows_other,
        acts,
        acts_other,
        hidden,
        hidden_other,
        grad_rows,
        grad_rows_other,
        squares,
        squares_other,
        in_specs=[SMEM] + [VMEM] * 10,
        out_specs=(ANY,) * 3 + (VMEM,) * 2,
        scratch_shapes=[pltpu.VMEM(value.shape, value.dtype) for value in (wide, wide, tall)]
        + [pltpu.SemaphoreType.DMA((6,))],
        flops=6 * token_count * width * units,
        vmem=24,
    )
    parts = spread_z(call(sum_kernel, (piece,) * Z, *slabs, after=(done,)))
    (grad_in,) = call(sum_kernel, (piece,), *parts)
    return student, loss[0, 0], grad_gate, grad_up, grad_down, grad_in


def solution(mesh):
    return jax.shard_map(
        per_device,
        mesh=mesh,
        in_specs=(
            P("col", "row"),
            P("col", "row"),
            P("row", "col"),
            P("row", "col"),
            P("col", "row"),
            P(None, "row", "col"),
        ),
        out_specs=(
            P("col", "row"),
            P(),
            P("row", "col"),
            P("row", "col"),
            P("col", "row"),
            P("col", "row"),
        ),
        check_vma=False,
    )
```

```python
import functools

import jax
import jax.numpy as jnp
from jax import lax
from jax.experimental import pallas as pl
from jax.experimental.pallas import tpu as pltpu
from jax.sharding import PartitionSpec as P

D = 8192
BLK = 128
X, Z, CORES = 4, 4, 2
CHIPS = X * Z
ROWS = 8
TILE = 512
DOWN = 2
SAME_CORE = [[chip * CORES + core for chip in range(CHIPS)] for core in range(CORES)]
VMEM = pl.BlockSpec(memory_space=pltpu.VMEM)
SMEM = pl.BlockSpec(memory_space=pltpu.SMEM)
ANY = pl.BlockSpec(memory_space=pl.ANY)


def call(kernel, shapes, *args, flops=0, vmem=12, in_specs=None, after=(), beside=False, **kwargs):
    moved = sum(a.size * a.dtype.itemsize for a in args)
    moved += sum(s.size * s.dtype.itemsize for s in jax.tree.leaves(shapes))
    return pl.pallas_call(
        lambda *refs: kernel(*refs[: len(args)], *refs[len(args) + len(after) :]),
        out_shape=shapes,
        in_specs=(in_specs or [VMEM] * len(args)) + [ANY] * len(after),
        compiler_params=pltpu.CompilerParams(vmem_limit_bytes=vmem << 20),
        cost_estimate=pl.CostEstimate(
            flops=0 if beside else flops, bytes_accessed=0 if beside else moved, transcendentals=0
        ),
        **kwargs,
    )(*args, *after)


def shaped(shape, dtype=jnp.bfloat16):
    return jax.ShapeDtypeStruct(shape, dtype)


DONE = shaped((8, BLK), jnp.float32)


def join_kernel(*refs):
    joined_ref = refs[-1]
    size = refs[0].shape[0]
    for part, ref in enumerate(refs[:-1]):
        joined_ref[pl.ds(part * size, size), :] = ref[...]


def keep_kernel(mask_ref, mask_other_ref, *refs):
    step = pl.program_id(0)
    gate_ups_ref, downs_ref = refs[-2:]
    for at, ref in enumerate(refs[:-2]):
        masks, which = (mask_ref, mask_other_ref)[at % 2], at // 2
        kept_ref = downs_ref.at[at % 2] if which == DOWN else gate_ups_ref.at[at]
        for col in range(ref.shape[1] // BLK):
            block = (step // 2, col) if which == DOWN else (col, step)
            factor = masks[which, block[0], block[1]].astype(jnp.float32).astype(jnp.bfloat16)
            cols = pl.ds(col * BLK, BLK)
            kept_ref[:, cols] = ref[:, cols] * factor


def keep(masks, weights):
    steps = weights[0].shape[0] // BLK
    kept = [shaped((count,) + value.shape) for count, value in ((4, weights[0]), (2, weights[-1]))]
    return call(
        keep_kernel,
        kept,
        *masks,
        *weights,
        in_specs=[SMEM] * 2
        + [pl.BlockSpec((value.shape[0] // steps, value.shape[1]), lambda i: (i, 0)) for value in weights],
        out_specs=[
            pl.BlockSpec((value.shape[0], value.shape[1] // steps, value.shape[2]), lambda i: (0, i, 0))
            for value in kept
        ],
        grid=(steps,),
        vmem=59,
    )


def plain_dot(left, right):
    return jnp.dot(left, right, preferred_element_type=jnp.float32)


def other_turned_dot(left, right):
    return lax.dot_general(left, right, (((1,), (1,)), ((), ())), preferred_element_type=jnp.float32)


def gate_up_kernel(chips_ref, weights_ref, out_ref, rows_ref, scratch, sems):
    copies = [
        pltpu.make_async_copy(weights_ref.at[which], scratch.at[which], sems.at[which])
        for which in range(weights_ref.shape[0])
    ]
    for copy in copies:
        copy.start()
    chip = lax.axis_index("col") // CORES
    size = chips_ref.shape[1]
    for part in range(CHIPS):
        x = lax.rem(chip // Z + part // Z, X)
        z = lax.rem(chip + part % Z, Z)
        rows_ref[pl.ds(part * size, size), :] = chips_ref[x * Z + z]
    for which, copy in enumerate(copies):
        units = scratch.shape[2]
        copy.wait()
        value = plain_dot(rows_ref[...], scratch[which])
        out_ref[:, pl.ds(which * units, units)] = value.astype(out_ref.dtype)


def put_slabs(out_refs, cols, value):
    size = out_refs[0].shape[0]
    for part, ref in enumerate(out_refs):
        ref[:, cols] = value[part * size : (part + 1) * size].astype(ref.dtype)


def output_kernel(hidden_ref, downs_ref, *out_refs):
    _, units, width = downs_ref.shape
    for at in range(0, width, TILE):
        cols = pl.ds(at, TILE)
        value = plain_dot(hidden_ref[:, :units], downs_ref[0, :, cols])
        value = value + plain_dot(hidden_ref[:, units:], downs_ref[1, :, cols])
        put_slabs(out_refs, cols, value)


def grad_hidden_kernel(*refs):
    slabs, (downs_ref, out_ref, grad_ref) = refs[:X], refs[X:]
    join_kernel(*slabs, grad_ref)
    units = downs_ref.shape[1]
    squares = jnp.sum(jnp.square(grad_ref[...].astype(jnp.float32)), axis=0, keepdims=True)
    squares = jnp.sum(squares, axis=1, keepdims=True)
    lane = lax.broadcasted_iota(jnp.int32, (out_ref.shape[0], BLK), 1)
    terms = jnp.zeros(lane.shape, jnp.float32)
    for which in range(3):
        term = squares.astype(jnp.bfloat16).astype(jnp.float32)
        terms = jnp.where(lane == which, term, terms)
        squares = squares - term
    out_ref[:, pl.ds(2 * units, BLK)] = terms.astype(out_ref.dtype)
    for which in range(2):
        value = other_turned_dot(grad_ref[...], downs_ref[which])
        out_ref[:, pl.ds(which * units, units)] = value.astype(out_ref.dtype)


def grad_in_kernel(acts_ref, weights_ref, *out_refs):
    count, width, units = weights_ref.shape
    for at in range(0, width, TILE):
        value = None
        for which in range(count):
            weight = weights_ref[which, pl.ds(at, TILE), :]
            term = other_turned_dot(acts_ref[:, pl.ds(which * units, units)], weight)
            value = term if value is None else value + term
        put_slabs(out_refs, pl.ds(at, TILE), value)


def multiply(kernel, shapes, left, weights, after=()):
    flops = 2 * sum(part.size // part.shape[-1] for part in left) * sum(weight.size for weight in weights)
    return call(kernel, shapes, *left, *weights, flops=flops, vmem=16, after=after)


def summed(parts):
    total = parts[0][...].astype(jnp.float32)
    for part in parts[1:]:
        total = total + part[...].astype(jnp.float32)
    return total


def parts_of(parts_ref):
    return [parts_ref.at[part] for part in range(parts_ref.shape[0])]


def hidden_kernel(parts_ref, both_ref, copies_ref):
    both = summed(parts_of(parts_ref))
    half = both.shape[1] // 2
    gate, up = both[:, :half], both[:, half:]
    hidden = (gate * jax.nn.sigmoid(gate) * up).astype(jnp.bfloat16)
    both_ref[...] = both
    for part in range(copies_ref.shape[0]):
        copies_ref[part] = hidden


def error_kernel(scale, teacher_ref, *refs):
    parts, (student_ref, grad_ref) = refs[:-2], refs[-2:]
    output = summed(parts)
    student_ref[...] = output.astype(jnp.bfloat16)
    grad_ref[...] = ((output - teacher_ref[...].astype(jnp.float32)) / scale).astype(jnp.bfloat16)


def acts_kernel(parts_ref, both_ref, copies_ref, squares_ref):
    total = summed(parts_of(parts_ref))
    half = both_ref.shape[1] // 2
    grad_hidden = total[:, :half]
    squares_ref[...] = jnp.broadcast_to(jnp.sum(total[:1, half:], axis=1, keepdims=True), squares_ref.shape)
    gate, up = both_ref[:, :half], both_ref[:, half:]
    sig = jax.nn.sigmoid(gate)
    grad_gate_act = (grad_hidden * up * sig * (1.0 + gate * (1.0 - sig))).astype(jnp.bfloat16)
    grad_up_act = (grad_hidden * (gate * sig)).astype(jnp.bfloat16)
    for part in range(copies_ref.shape[0]):
        copies_ref[part, :, :half] = grad_gate_act
        copies_ref[part, :, half:] = grad_up_act


def sum_kernel(*refs):
    parts, out_refs = refs[:X], refs[X:]
    put_slabs(out_refs, slice(None), summed(parts))


def put_kept(mask_ref, which, value, col, scratch_ref):
    for row in range(value.shape[0] // BLK):
        for step in range(value.shape[1] // BLK):
            at = (row, col + step) if which == DOWN else (col + step, row)
            factor = mask_ref[which, at[0], at[1]].astype(jnp.float32)
            block = value[row * BLK : (row + 1) * BLK, step * BLK : (step + 1) * BLK] * factor
            scratch_ref[pl.ds(row * BLK, BLK), pl.ds((col + step) * BLK, BLK)] = block.astype(jnp.bfloat16)


def weights_kernel(
    mask_ref,
    rows_ref,
    rows_other_ref,
    acts_ref,
    acts_other_ref,
    hidden_ref,
    hidden_other_ref,
    grad_ref,
    grad_other_ref,
    squares_ref,
    squares_other_ref,
    gate_ref,
    up_ref,
    down_ref,
    loss_ref,
    done_ref,
    gate_scratch,
    up_scratch,
    down_scratch,
    sems,
):
    units = gate_ref.shape[1]
    loss_ref[...] = (squares_ref[:1, :1] + squares_other_ref[:1, :1]) * (1.0 / D)
    done_ref[...] = jnp.zeros_like(done_ref)
    copies = []

    def put(which, value, col, scratch, out_ref):
        put_kept(mask_ref, which, value, col, scratch)
        cols = pl.ds(col * BLK, value.shape[1])
        copy = pltpu.make_async_copy(scratch.at[:, cols], out_ref.at[:, cols], sems.at[len(copies)])
        copy.start()
        copies.append(copy)

    turned, turned_other = hidden_ref[:, :units].T, hidden_other_ref[:, units:].T
    for col in range(0, down_ref.shape[1] // BLK, 4):
        cols = pl.ds(col * BLK, 4 * BLK)
        value = plain_dot(turned, grad_ref[:, cols]) + plain_dot(turned_other, grad_other_ref[:, cols])
        put(DOWN, value, col, down_scratch, down_ref)
    turned, turned_other = rows_ref[...].T, rows_other_ref[...].T
    for which, (scratch, out_ref) in enumerate(((gate_scratch, gate_ref), (up_scratch, up_ref))):
        for col in range(0, units // BLK, 2):
            own = pl.ds(2 * which * units + col * BLK, 2 * BLK)
            other = pl.ds((2 * which + 1) * units + col * BLK, 2 * BLK)
            value = plain_dot(turned, acts_ref[:, own]) + plain_dot(turned_other, acts_other_ref[:, other])
            put(which, value, col, scratch, out_ref)
    for copy in copies:
        copy.wait()


def other_core(value):
    count = CHIPS * CORES
    return lax.ppermute(value, "col", [(device, device ^ 1) for device in range(count)])


def fetch(value, dx, dz):
    pairs = [
        ((((x + dx) % X * Z + (z + dz) % Z) * CORES + core), (x * Z + z) * CORES + core)
        for x in range(X)
        for z in range(Z)
        for core in range(CORES)
    ]
    return lax.ppermute(value, "col", pairs)


def gather_z(block):
    return [block] + [fetch(block, 0, step) for step in range(1, Z)]


def joined(parts):
    size, width = parts[0].shape
    return call(join_kernel, shaped((len(parts) * size, width)), *parts)


def gather_x(block):
    return [block] + [fetch(block, step, 0) for step in range(1, X)]


def spread_x(parts):
    return [parts[0]] + [fetch(parts[step], -step, 0) for step in range(1, X)]


def spread_z(parts):
    return [parts[0]] + [fetch(parts[step], 0, -step) for step in range(1, Z)]


def exchange_row(value):
    return lax.all_to_all(value, "row", 0, 0)


def flat(value):
    return value.reshape((-1,) + value.shape[2:])


def split(value, count):
    return value.reshape((count, -1) + value.shape[1:])


def per_device(inputs, teacher, gate_weight, up_weight, down_weight, block_mask):
    tokens, width = inputs.shape
    token_count = tokens * CHIPS * CORES
    units = gate_weight.shape[1]
    half = tokens * CHIPS
    scale = float(token_count) ** 0.5
    mask = jnp.transpose(block_mask, (0, 2, 1))
    slab = shaped((Z * tokens, width))
    piece = shaped((tokens, width))
    wide, tall = shaped((width, units)), shaped((units, width))
    gates, ups, downs, masks = (
        (value, other_core(value)) for value in (gate_weight, up_weight, down_weight, mask)
    )
    copies = jnp.broadcast_to(inputs[None], (CHIPS, tokens, width))
    chips = lax.all_to_all(copies, "col", 0, 0, axis_index_groups=SAME_CORE)
    gate_ups, downs = keep(masks, gates + ups + downs)
    partial, rows = call(
        gate_up_kernel,
        (shaped((half, 4 * units)), shaped((half, width))),
        chips,
        gate_ups,
        in_specs=[VMEM, ANY],
        scratch_shapes=[pltpu.VMEM(gate_ups.shape, gate_ups.dtype), pltpu.SemaphoreType.DMA((4,))],
        flops=8 * half * width * units,
        vmem=60,
    )
    both, copies = call(
        hidden_kernel,
        (shaped((half // ROWS, 4 * units), jnp.float32), shaped((ROWS, half // ROWS, 2 * units))),
        exchange_row(split(partial, ROWS)),
    )
    hidden = flat(exchange_row(copies))
    slabs = spread_x(multiply(output_kernel, (slab,) * X, [hidden], [downs]))
    rows_other, hidden_other = other_core(rows), other_core(hidden)
    parts = spread_z(call(sum_kernel, (piece,) * Z, *slabs))
    student, grad_out = call(functools.partial(error_kernel, scale), (piece, piece), teacher, *parts)
    slabs = gather_x(joined(gather_z(grad_out)))
    partial, grad_rows = multiply(
        grad_hidden_kernel, (shaped((half, 2 * units + BLK)), shaped((half, width))), slabs, [downs], (rows_other, hidden_other)
    )
    copies, squares = call(
        acts_kernel,
        (shaped((ROWS, half // ROWS, 4 * units)), DONE),
        exchange_row(split(partial, ROWS)),
        both,
    )
    acts = flat(exchange_row(copies))
    slabs = spread_x(multiply(grad_in_kernel, (slab,) * X, [acts], [gate_ups]))
    grad_rows_other, acts_other, squares_other = (other_core(value) for value in (grad_rows, acts, squares))
    grad_gate, grad_up, grad_down, loss, done = call(
        weights_kernel,
        (wide, wide, tall, shaped((1, 1), jnp.float32), DONE),
        mask,
        rows,
        rows_other,
        acts,
        acts_other,
        hidden,
        hidden_other,
        grad_rows,
        grad_rows_other,
        squares,
        squares_other,
        in_specs=[SMEM] + [VMEM] * 10,
        out_specs=(ANY,) * 3 + (VMEM,) * 2,
        scratch_shapes=[pltpu.VMEM(value.shape, value.dtype) for value in (wide, wide, tall)]
        + [pltpu.SemaphoreType.DMA((6,))],
        flops=6 * token_count * width * units,
        vmem=24,
    )
    parts = spread_z(call(sum_kernel, (piece,) * Z, *slabs, after=(done,)))
    (grad_in,) = call(sum_kernel, (piece,), *parts)
    return student, loss[0, 0], grad_gate, grad_up, grad_down, grad_in


def solution(mesh):
    return jax.shard_map(
        per_device,
        mesh=mesh,
        in_specs=(
            P("col", "row"),
            P("col", "row"),
            P("row", "col"),
            P("row", "col"),
            P("col", "row"),
            P(None, "row", "col"),
        ),
        out_specs=(
            P("col", "row"),
            P(),
            P("row", "col"),
            P("row", "col"),
            P("col", "row"),
            P("col", "row"),
        ),
        check_vma=False,
    )
```

```python
import functools

import jax
import jax.numpy as jnp
from jax import lax
from jax.experimental import pallas as pl
from jax.experimental.pallas import tpu as pltpu
from jax.sharding import PartitionSpec as P

D = 8192
BLK = 128
X, Z, CORES = 4, 4, 2
CHIPS = X * Z
ROWS = 8
TILE = 512
DOWN = 2
SAME_CORE = [[chip * CORES + core for chip in range(CHIPS)] for core in range(CORES)]
VMEM = pl.BlockSpec(memory_space=pltpu.VMEM)
SMEM = pl.BlockSpec(memory_space=pltpu.SMEM)
ANY = pl.BlockSpec(memory_space=pl.ANY)


def call(kernel, shapes, *args, flops=0, vmem=12, in_specs=None, after=(), beside=False, **kwargs):
    moved = sum(a.size * a.dtype.itemsize for a in args)
    moved += sum(s.size * s.dtype.itemsize for s in jax.tree.leaves(shapes))
    return pl.pallas_call(
        lambda *refs: kernel(*refs[: len(args)], *refs[len(args) + len(after) :]),
        out_shape=shapes,
        in_specs=(in_specs or [VMEM] * len(args)) + [ANY] * len(after),
        compiler_params=pltpu.CompilerParams(vmem_limit_bytes=vmem << 20),
        cost_estimate=pl.CostEstimate(
            flops=0 if beside else flops, bytes_accessed=0 if beside else moved, transcendentals=0
        ),
        **kwargs,
    )(*args, *after)


def shaped(shape, dtype=jnp.bfloat16):
    return jax.ShapeDtypeStruct(shape, dtype)


DONE = shaped((8, BLK), jnp.float32)


def join_kernel(*refs):
    joined_ref = refs[-1]
    size = refs[0].shape[0]
    for part, ref in enumerate(refs[:-1]):
        joined_ref[pl.ds(part * size, size), :] = ref[...]


def fetched(pairs, sems):
    copies = [pltpu.make_async_copy(src, dst, sems.at[at]) for at, (src, dst) in enumerate(pairs)]
    for copy in copies:
        copy.start()
    return copies


def keep_kernel(mask_ref, mask_other_ref, *refs):
    raw_refs, kept_refs, scratches, sems = refs[:6], refs[6:12], refs[12:18], refs[18]
    for at, copy in enumerate(fetched(zip(raw_refs, scratches), sems)):
        masks, which = (mask_ref, mask_other_ref)[at % 2], at // 2
        copy.wait()
        for row in range(raw_refs[at].shape[0] // BLK):
            for col in range(raw_refs[at].shape[1] // BLK):
                block = (row, col) if which == DOWN else (col, row)
                factor = masks[which, block[0], block[1]].astype(jnp.float32).astype(jnp.bfloat16)
                place = (pl.ds(row * BLK, BLK), pl.ds(col * BLK, BLK))
                kept_refs[at][place] = scratches[at][place] * factor


def keep(masks, weights):
    return call(
        keep_kernel,
        [shaped(value.shape) for value in weights],
        *masks,
        *weights,
        in_specs=[SMEM] * 2 + [ANY] * 6,
        scratch_shapes=[pltpu.VMEM(value.shape, value.dtype) for value in weights]
        + [pltpu.SemaphoreType.DMA((6,))],
        vmem=24,
    )


def plain_dot(left, right):
    return jnp.dot(left, right, preferred_element_type=jnp.float32)


def other_turned_dot(left, right):
    return lax.dot_general(left, right, (((1,), (1,)), ((), ())), preferred_element_type=jnp.float32)


def gate_up_kernel(chips_ref, *refs):
    weights, (out_ref, rows_ref, sems) = refs[:4], refs[4:]
    chip = lax.axis_index("col") // CORES
    size = chips_ref.shape[1]
    pairs = []
    for part in range(CHIPS):
        x = lax.rem(chip // Z + part // Z, X)
        z = lax.rem(chip + part % Z, Z)
        pairs.append((chips_ref.at[x * Z + z], rows_ref.at[pl.ds(part * size, size), :]))
    for copy in fetched(pairs, sems):
        copy.wait()
    for which, ref in enumerate(weights):
        units = ref.shape[1]
        value = plain_dot(rows_ref[...], ref[...])
        out_ref[:, pl.ds(which * units, units)] = value.astype(out_ref.dtype)


def put_slabs(out_refs, cols, value):
    size = out_refs[0].shape[0]
    for part, ref in enumerate(out_refs):
        ref[:, cols] = value[part * size : (part + 1) * size].astype(ref.dtype)


def output_kernel(hidden_ref, down_ref, down_other_ref, *out_refs):
    units, width = down_ref.shape
    for at in range(0, width, TILE):
        cols = pl.ds(at, TILE)
        value = plain_dot(hidden_ref[:, :units], down_ref[:, cols])
        value = value + plain_dot(hidden_ref[:, units:], down_other_ref[:, cols])
        put_slabs(out_refs, cols, value)


def grad_hidden_kernel(*refs):
    slabs, (down_ref, down_other_ref, out_ref, grad_ref) = refs[:X], refs[X:]
    join_kernel(*slabs, grad_ref)
    units = down_ref.shape[0]
    squares = jnp.sum(jnp.square(grad_ref[...].astype(jnp.float32)), axis=0, keepdims=True)
    squares = jnp.sum(squares, axis=1, keepdims=True)
    lane = lax.broadcasted_iota(jnp.int32, (out_ref.shape[0], BLK), 1)
    terms = jnp.zeros(lane.shape, jnp.float32)
    for which in range(3):
        term = squares.astype(jnp.bfloat16).astype(jnp.float32)
        terms = jnp.where(lane == which, term, terms)
        squares = squares - term
    out_ref[:, pl.ds(2 * units, BLK)] = terms.astype(out_ref.dtype)
    for which, ref in enumerate((down_ref, down_other_ref)):
        value = other_turned_dot(grad_ref[...], ref[...])
        out_ref[:, pl.ds(which * units, units)] = value.astype(out_ref.dtype)


def grad_in_kernel(acts_ref, *refs):
    weights, out_refs = refs[:-X], refs[-X:]
    width, units = weights[0].shape
    for at in range(0, width, TILE):
        value = None
        for which, ref in enumerate(weights):
            term = other_turned_dot(acts_ref[:, pl.ds(which * units, units)], ref[pl.ds(at, TILE), :])
            value = term if value is None else value + term
        put_slabs(out_refs, pl.ds(at, TILE), value)


def multiply(kernel, shapes, left, weights, after=()):
    flops = 2 * sum(part.size // part.shape[-1] for part in left) * sum(weight.size for weight in weights)
    return call(kernel, shapes, *left, *weights, flops=flops, vmem=16, after=after)


def summed(parts):
    total = parts[0][...].astype(jnp.float32)
    for part in parts[1:]:
        total = total + part[...].astype(jnp.float32)
    return total


def parts_of(parts_ref):
    return [parts_ref.at[part] for part in range(parts_ref.shape[0])]


def hidden_kernel(sent_ref, both_ref, copies_ref, parts_ref, sems):
    for copy in fetched([(sent_ref.at[part], parts_ref.at[part]) for part in range(ROWS)], sems):
        copy.wait()
    both = summed(parts_of(parts_ref))
    half = both.shape[1] // 2
    gate, up = both[:, :half], both[:, half:]
    hidden = (gate * jax.nn.sigmoid(gate) * up).astype(jnp.bfloat16)
    both_ref[...] = both
    for part in range(copies_ref.shape[0]):
        copies_ref[part] = hidden


def error_kernel(scale, teacher_ref, *refs):
    parts, (student_ref, grad_ref) = refs[:-2], refs[-2:]
    output = summed(parts)
    student_ref[...] = output.astype(jnp.bfloat16)
    grad_ref[...] = ((output - teacher_ref[...].astype(jnp.float32)) / scale).astype(jnp.bfloat16)


def acts_kernel(parts_ref, both_ref, copies_ref, squares_ref):
    total = summed(parts_of(parts_ref))
    half = both_ref.shape[1] // 2
    grad_hidden = total[:, :half]
    squares_ref[...] = jnp.broadcast_to(jnp.sum(total[:1, half:], axis=1, keepdims=True), squares_ref.shape)
    gate, up = both_ref[:, :half], both_ref[:, half:]
    sig = jax.nn.sigmoid(gate)
    grad_gate_act = (grad_hidden * up * sig * (1.0 + gate * (1.0 - sig))).astype(jnp.bfloat16)
    grad_up_act = (grad_hidden * (gate * sig)).astype(jnp.bfloat16)
    for part in range(copies_ref.shape[0]):
        copies_ref[part, :, :half] = grad_gate_act
        copies_ref[part, :, half:] = grad_up_act


def sum_kernel(*refs):
    parts, out_refs = refs[:X], refs[X:]
    put_slabs(out_refs, slice(None), summed(parts))


def put_kept(mask_ref, which, value, col, scratch_ref):
    for row in range(value.shape[0] // BLK):
        for step in range(value.shape[1] // BLK):
            at = (row, col + step) if which == DOWN else (col + step, row)
            factor = mask_ref[which, at[0], at[1]].astype(jnp.float32)
            block = value[row * BLK : (row + 1) * BLK, step * BLK : (step + 1) * BLK] * factor
            scratch_ref[pl.ds(row * BLK, BLK), pl.ds((col + step) * BLK, BLK)] = block.astype(jnp.bfloat16)


def weights_kernel(
    mask_ref,
    rows_ref,
    rows_other_ref,
    acts_ref,
    acts_other_ref,
    hidden_ref,
    hidden_other_ref,
    grad_ref,
    grad_other_ref,
    squares_ref,
    squares_other_ref,
    gate_ref,
    up_ref,
    down_ref,
    loss_ref,
    done_ref,
    gate_scratch,
    up_scratch,
    down_scratch,
    sems,
):
    units = gate_ref.shape[1]
    loss_ref[...] = (squares_ref[:1, :1] + squares_other_ref[:1, :1]) * (1.0 / D)
    done_ref[...] = jnp.zeros_like(done_ref)
    copies = []

    def put(which, value, col, scratch, out_ref):
        put_kept(mask_ref, which, value, col, scratch)
        cols = pl.ds(col * BLK, value.shape[1])
        copy = pltpu.make_async_copy(scratch.at[:, cols], out_ref.at[:, cols], sems.at[len(copies)])
        copy.start()
        copies.append(copy)

    turned, turned_other = hidden_ref[:, :units].T, hidden_other_ref[:, units:].T
    for col in range(0, down_ref.shape[1] // BLK, 4):
        cols = pl.ds(col * BLK, 4 * BLK)
        value = plain_dot(turned, grad_ref[:, cols]) + plain_dot(turned_other, grad_other_ref[:, cols])
        put(DOWN, value, col, down_scratch, down_ref)
    turned, turned_other = rows_ref[...].T, rows_other_ref[...].T
    for which, (scratch, out_ref) in enumerate(((gate_scratch, gate_ref), (up_scratch, up_ref))):
        for col in range(0, units // BLK, 2):
            own = pl.ds(2 * which * units + col * BLK, 2 * BLK)
            other = pl.ds((2 * which + 1) * units + col * BLK, 2 * BLK)
            value = plain_dot(turned, acts_ref[:, own]) + plain_dot(turned_other, acts_other_ref[:, other])
            put(which, value, col, scratch, out_ref)
    for copy in copies:
        copy.wait()


def hold_kernel(*refs):
    pass


def hold(values, after):
    return pl.pallas_call(
        hold_kernel,
        out_shape=[shaped(value.shape) for value in values],
        in_specs=[ANY] * (len(values) + len(after)),
        out_specs=[ANY] * len(values),
        input_output_aliases={at: at for at in range(len(values))},
    )(*values, *after)


def other_core(value):
    count = CHIPS * CORES
    return lax.ppermute(value, "col", [(device, device ^ 1) for device in range(count)])


def fetch(value, dx, dz):
    pairs = [
        ((((x + dx) % X * Z + (z + dz) % Z) * CORES + core), (x * Z + z) * CORES + core)
        for x in range(X)
        for z in range(Z)
        for core in range(CORES)
    ]
    return lax.ppermute(value, "col", pairs)


def gather_z(block):
    return [block] + [fetch(block, 0, step) for step in range(1, Z)]


def joined(parts):
    size, width = parts[0].shape
    return call(join_kernel, shaped((len(parts) * size, width)), *parts)


def gather_x(block):
    return [block] + [fetch(block, step, 0) for step in range(1, X)]


def spread_x(parts):
    return [parts[0]] + [fetch(parts[step], -step, 0) for step in range(1, X)]


def spread_z(parts):
    return [parts[0]] + [fetch(parts[step], 0, -step) for step in range(1, Z)]


def exchange_row(value):
    return lax.all_to_all(value, "row", 0, 0)


def in_hbm(value):
    return pltpu.with_memory_space_constraint(value, pltpu.HBM)


def flat(value):
    return value.reshape((-1,) + value.shape[2:])


def split(value, count):
    return value.reshape((count, -1) + value.shape[1:])


def per_device(inputs, teacher, gate_weight, up_weight, down_weight, block_mask):
    tokens, width = inputs.shape
    token_count = tokens * CHIPS * CORES
    units = gate_weight.shape[1]
    half = tokens * CHIPS
    scale = float(token_count) ** 0.5
    mask = jnp.transpose(block_mask, (0, 2, 1))
    slab = shaped((Z * tokens, width))
    piece = shaped((tokens, width))
    wide, tall = shaped((width, units)), shaped((units, width))
    gates, ups, downs, masks = (
        (value, other_core(value)) for value in (gate_weight, up_weight, down_weight, mask)
    )
    copies = jnp.broadcast_to(inputs[None], (CHIPS, tokens, width))
    chips = lax.all_to_all(copies, "col", 0, 0, axis_index_groups=SAME_CORE)
    chips = in_hbm(chips)
    kept = keep(masks, [value for own, other in (gates, ups, downs) for value in (in_hbm(own), other)])
    gate_ups, downs = kept[:4], kept[4:]
    partial, rows = call(
        gate_up_kernel,
        (shaped((half, 4 * units)), shaped((half, width))),
        chips,
        *gate_ups,
        in_specs=[ANY] + [VMEM] * 4,
        scratch_shapes=[pltpu.SemaphoreType.DMA((CHIPS,))],
        flops=8 * half * width * units,
        vmem=16,
    )
    sent = in_hbm(exchange_row(split(partial, ROWS)))
    both, copies = call(
        hidden_kernel,
        (shaped((half // ROWS, 4 * units), jnp.float32), shaped((ROWS, half // ROWS, 2 * units))),
        sent,
        in_specs=[ANY],
        scratch_shapes=[pltpu.VMEM(sent.shape, sent.dtype), pltpu.SemaphoreType.DMA((ROWS,))],
    )
    hidden = flat(exchange_row(copies))
    slabs = spread_x(multiply(output_kernel, (slab,) * X, [hidden], downs))
    parts = call(sum_kernel, (piece,) * Z, *slabs)
    rows, hidden = hold((rows, hidden), parts[:1])
    rows_other, hidden_other = other_core(rows), other_core(hidden)
    parts = spread_z(parts)
    student, grad_out = call(functools.partial(error_kernel, scale), (piece, piece), teacher, *parts)
    slabs = gather_x(joined(gather_z(grad_out)))
    partial, grad_rows = multiply(
        grad_hidden_kernel, (shaped((half, 2 * units + BLK)), shaped((half, width))), slabs, downs, (rows_other, hidden_other)
    )
    copies, squares = call(
        acts_kernel,
        (shaped((ROWS, half // ROWS, 4 * units)), DONE),
        exchange_row(split(partial, ROWS)),
        both,
    )
    acts = flat(exchange_row(copies))
    slabs = spread_x(multiply(grad_in_kernel, (slab,) * X, [acts], gate_ups))
    grad_rows_other, acts_other, squares_other = (other_core(value) for value in (grad_rows, acts, squares))
    grad_gate, grad_up, grad_down, loss, done = call(
        weights_kernel,
        (wide, wide, tall, shaped((1, 1), jnp.float32), DONE),
        mask,
        rows,
        rows_other,
        acts,
        acts_other,
        hidden,
        hidden_other,
        grad_rows,
        grad_rows_other,
        squares,
        squares_other,
        in_specs=[SMEM] + [VMEM] * 10,
        out_specs=(ANY,) * 3 + (VMEM,) * 2,
        scratch_shapes=[pltpu.VMEM(value.shape, value.dtype) for value in (wide, wide, tall)]
        + [pltpu.SemaphoreType.DMA((6,))],
        flops=6 * token_count * width * units,
        vmem=24,
    )
    parts = spread_z(call(sum_kernel, (piece,) * Z, *slabs, after=(done,)))
    (grad_in,) = call(sum_kernel, (piece,), *parts)
    return student, loss[0, 0], grad_gate, grad_up, grad_down, grad_in


def solution(mesh):
    return jax.shard_map(
        per_device,
        mesh=mesh,
        in_specs=(
            P("col", "row"),
            P("col", "row"),
            P("row", "col"),
            P("row", "col"),
            P("col", "row"),
            P(None, "row", "col"),
        ),
        out_specs=(
            P("col", "row"),
            P(),
            P("row", "col"),
            P("row", "col"),
            P("col", "row"),
            P("col", "row"),
        ),
        check_vma=False,
    )
```

```python
import functools

import jax
import jax.numpy as jnp
from jax import lax
from jax.experimental import pallas as pl
from jax.experimental.pallas import tpu as pltpu
from jax.sharding import PartitionSpec as P

D = 8192
BLK = 128
X, Z, CORES = 4, 4, 2
CHIPS = X * Z
ROWS = 8
TILE = 512
DOWN = 2
SAME_CORE = [[chip * CORES + core for chip in range(CHIPS)] for core in range(CORES)]
VMEM = pl.BlockSpec(memory_space=pltpu.VMEM)
SMEM = pl.BlockSpec(memory_space=pltpu.SMEM)
ANY = pl.BlockSpec(memory_space=pl.ANY)


def call(kernel, shapes, *args, flops=0, vmem=12, in_specs=None, after=(), beside=False, **kwargs):
    moved = sum(a.size * a.dtype.itemsize for a in args)
    moved += sum(s.size * s.dtype.itemsize for s in jax.tree.leaves(shapes))
    return pl.pallas_call(
        lambda *refs: kernel(*refs[: len(args)], *refs[len(args) + len(after) :]),
        out_shape=shapes,
        in_specs=(in_specs or [VMEM] * len(args)) + [ANY] * len(after),
        compiler_params=pltpu.CompilerParams(vmem_limit_bytes=vmem << 20),
        cost_estimate=pl.CostEstimate(
            flops=0 if beside else flops, bytes_accessed=0 if beside else moved, transcendentals=0
        ),
        **kwargs,
    )(*args, *after)


def shaped(shape, dtype=jnp.bfloat16):
    return jax.ShapeDtypeStruct(shape, dtype)


DONE = shaped((8, BLK), jnp.float32)


def join_kernel(*refs):
    joined_ref = refs[-1]
    size = refs[0].shape[0]
    for part, ref in enumerate(refs[:-1]):
        joined_ref[pl.ds(part * size, size), :] = ref[...]


def keep(mask_ref, which, ref, kept_ref):
    for row in range(ref.shape[0] // BLK):
        for col in range(ref.shape[1] // BLK):
            at = (row, col) if which == DOWN else (col, row)
            factor = mask_ref[which, at[0], at[1]].astype(jnp.float32).astype(jnp.bfloat16)
            block = (pl.ds(row * BLK, BLK), pl.ds(col * BLK, BLK))
            kept_ref[block] = ref[block] * factor


def plain_dot(left, right):
    return jnp.dot(left, right, preferred_element_type=jnp.float32)


def other_turned_dot(left, right):
    return lax.dot_general(left, right, (((1,), (1,)), ((), ())), preferred_element_type=jnp.float32)


def gate_up_kernel(mask_ref, mask_other_ref, chips_ref, *refs):
    weights, kept_refs, (out_ref, rows_ref, scratch, sems) = list(refs[:4]), refs[4:8], refs[8:]
    chip = lax.axis_index("col") // CORES
    size = chips_ref.shape[1]
    pairs = [(weights[2], scratch)]
    for part in range(CHIPS):
        x = lax.rem(chip // Z + part // Z, X)
        z = lax.rem(chip + part % Z, Z)
        pairs.append((chips_ref.at[x * Z + z], rows_ref.at[pl.ds(part * size, size), :]))
    copies = [pltpu.make_async_copy(src, dst, sems.at[at]) for at, (src, dst) in enumerate(pairs)]
    for copy in copies[1:] + copies[:1]:
        copy.start()
    weights[2] = scratch

    def masked(which):
        keep((mask_ref, mask_other_ref)[which % 2], which // 2, weights[which], kept_refs[which])

    def multiplied(which):
        units = scratch.shape[1]
        value = plain_dot(rows_ref[...], kept_refs[which][...])
        out_ref[:, pl.ds(which * units, units)] = value.astype(out_ref.dtype)

    for which in (0, 1, 3):
        masked(which)
    for copy in copies[1:]:
        copy.wait()
    for which in (0, 1, 3):
        multiplied(which)
    copies[0].wait()
    masked(2)
    multiplied(2)


def put_slabs(out_refs, cols, value):
    size = out_refs[0].shape[0]
    for part, ref in enumerate(out_refs):
        ref[:, cols] = value[part * size : (part + 1) * size].astype(ref.dtype)


def output_kernel(mask_ref, mask_other_ref, hidden_ref, down_ref, down_other_ref, kept_ref, kept_other_ref, *out_refs):
    units, width = down_ref.shape
    keep(mask_ref, DOWN, down_ref, kept_ref)
    keep(mask_other_ref, DOWN, down_other_ref, kept_other_ref)
    for at in range(0, width, TILE):
        cols = pl.ds(at, TILE)
        value = plain_dot(hidden_ref[:, :units], kept_ref[:, cols])
        value = value + plain_dot(hidden_ref[:, units:], kept_other_ref[:, cols])
        put_slabs(out_refs, cols, value)


def grad_hidden_kernel(*refs):
    slabs, (down_ref, down_other_ref, out_ref, grad_ref) = refs[:X], refs[X:]
    join_kernel(*slabs, grad_ref)
    units = down_ref.shape[0]
    squares = jnp.sum(jnp.square(grad_ref[...].astype(jnp.float32)), axis=0, keepdims=True)
    squares = jnp.sum(squares, axis=1, keepdims=True)
    lane = lax.broadcasted_iota(jnp.int32, (out_ref.shape[0], BLK), 1)
    terms = jnp.zeros(lane.shape, jnp.float32)
    for which in range(3):
        term = squares.astype(jnp.bfloat16).astype(jnp.float32)
        terms = jnp.where(lane == which, term, terms)
        squares = squares - term
    out_ref[:, pl.ds(2 * units, BLK)] = terms.astype(out_ref.dtype)
    for which, ref in enumerate((down_ref, down_other_ref)):
        value = other_turned_dot(grad_ref[...], ref[...])
        out_ref[:, pl.ds(which * units, units)] = value.astype(out_ref.dtype)


def grad_in_kernel(acts_ref, *refs):
    weights, out_refs = refs[:-X], refs[-X:]
    width, units = weights[0].shape
    for at in range(0, width, TILE):
        value = None
        for which, ref in enumerate(weights):
            term = other_turned_dot(acts_ref[:, pl.ds(which * units, units)], ref[pl.ds(at, TILE), :])
            value = term if value is None else value + term
        put_slabs(out_refs, pl.ds(at, TILE), value)


def multiply(kernel, shapes, left, weights, masks=(), after=()):
    flops = 2 * sum(part.size // part.shape[-1] for part in left) * sum(weight.size for weight in weights)
    specs = [SMEM] * len(masks) + [VMEM] * (len(left) + len(weights))
    return call(kernel, shapes, *masks, *left, *weights, flops=flops, vmem=16, in_specs=specs, after=after)


def summed(parts):
    total = parts[0][...].astype(jnp.float32)
    for part in parts[1:]:
        total = total + part[...].astype(jnp.float32)
    return total


def parts_of(parts_ref):
    return [parts_ref.at[part] for part in range(parts_ref.shape[0])]


def hidden_kernel(parts_ref, both_ref, copies_ref):
    both = summed(parts_of(parts_ref))
    half = both.shape[1] // 2
    gate, up = both[:, :half], both[:, half:]
    hidden = (gate * jax.nn.sigmoid(gate) * up).astype(jnp.bfloat16)
    both_ref[...] = both
    for part in range(copies_ref.shape[0]):
        copies_ref[part] = hidden


def error_kernel(scale, teacher_ref, *refs):
    parts, (student_ref, grad_ref) = refs[:-2], refs[-2:]
    output = summed(parts)
    student_ref[...] = output.astype(jnp.bfloat16)
    grad_ref[...] = ((output - teacher_ref[...].astype(jnp.float32)) / scale).astype(jnp.bfloat16)


def acts_kernel(parts_ref, both_ref, copies_ref, squares_ref):
    total = summed(parts_of(parts_ref))
    half = both_ref.shape[1] // 2
    grad_hidden = total[:, :half]
    squares_ref[...] = jnp.broadcast_to(jnp.sum(total[:1, half:], axis=1, keepdims=True), squares_ref.shape)
    gate, up = both_ref[:, :half], both_ref[:, half:]
    sig = jax.nn.sigmoid(gate)
    grad_gate_act = (grad_hidden * up * sig * (1.0 + gate * (1.0 - sig))).astype(jnp.bfloat16)
    grad_up_act = (grad_hidden * (gate * sig)).astype(jnp.bfloat16)
    for part in range(copies_ref.shape[0]):
        copies_ref[part, :, :half] = grad_gate_act
        copies_ref[part, :, half:] = grad_up_act


def sum_kernel(*refs):
    parts, out_refs = refs[:X], refs[X:]
    put_slabs(out_refs, slice(None), summed(parts))


def put_kept(mask_ref, which, value, col, scratch_ref):
    for row in range(value.shape[0] // BLK):
        for step in range(value.shape[1] // BLK):
            at = (row, col + step) if which == DOWN else (col + step, row)
            factor = mask_ref[which, at[0], at[1]].astype(jnp.float32)
            block = value[row * BLK : (row + 1) * BLK, step * BLK : (step + 1) * BLK] * factor
            scratch_ref[pl.ds(row * BLK, BLK), pl.ds((col + step) * BLK, BLK)] = block.astype(jnp.bfloat16)


def weights_kernel(
    mask_ref,
    rows_ref,
    rows_other_ref,
    acts_ref,
    acts_other_ref,
    hidden_ref,
    hidden_other_ref,
    grad_ref,
    grad_other_ref,
    squares_ref,
    squares_other_ref,
    gate_ref,
    up_ref,
    down_ref,
    loss_ref,
    done_ref,
    gate_scratch,
    up_scratch,
    down_scratch,
    sems,
):
    units = gate_ref.shape[1]
    loss_ref[...] = (squares_ref[:1, :1] + squares_other_ref[:1, :1]) * (1.0 / D)
    done_ref[...] = jnp.zeros_like(done_ref)
    copies = []

    def put(which, value, col, scratch, out_ref):
        put_kept(mask_ref, which, value, col, scratch)
        cols = pl.ds(col * BLK, value.shape[1])
        copy = pltpu.make_async_copy(scratch.at[:, cols], out_ref.at[:, cols], sems.at[len(copies)])
        copy.start()
        copies.append(copy)

    turned, turned_other = hidden_ref[:, :units].T, hidden_other_ref[:, units:].T
    for col in range(0, down_ref.shape[1] // BLK, 4):
        cols = pl.ds(col * BLK, 4 * BLK)
        value = plain_dot(turned, grad_ref[:, cols]) + plain_dot(turned_other, grad_other_ref[:, cols])
        put(DOWN, value, col, down_scratch, down_ref)
    turned, turned_other = rows_ref[...].T, rows_other_ref[...].T
    for which, (scratch, out_ref) in enumerate(((gate_scratch, gate_ref), (up_scratch, up_ref))):
        for col in range(0, units // BLK, 2):
            own = pl.ds(2 * which * units + col * BLK, 2 * BLK)
            other = pl.ds((2 * which + 1) * units + col * BLK, 2 * BLK)
            value = plain_dot(turned, acts_ref[:, own]) + plain_dot(turned_other, acts_other_ref[:, other])
            put(which, value, col, scratch, out_ref)
    for copy in copies:
        copy.wait()


def other_core(value):
    count = CHIPS * CORES
    return lax.ppermute(value, "col", [(device, device ^ 1) for device in range(count)])


def fetch(value, dx, dz):
    pairs = [
        ((((x + dx) % X * Z + (z + dz) % Z) * CORES + core), (x * Z + z) * CORES + core)
        for x in range(X)
        for z in range(Z)
        for core in range(CORES)
    ]
    return lax.ppermute(value, "col", pairs)


def gather_z(block):
    return [block] + [fetch(block, 0, step) for step in range(1, Z)]


def joined(parts):
    size, width = parts[0].shape
    return call(join_kernel, shaped((len(parts) * size, width)), *parts)


def gather_x(block):
    return [block] + [fetch(block, step, 0) for step in range(1, X)]


def spread_x(parts):
    return [parts[0]] + [fetch(parts[step], -step, 0) for step in range(1, X)]


def spread_z(parts):
    return [parts[0]] + [fetch(parts[step], 0, -step) for step in range(1, Z)]


def exchange_row(value):
    return lax.all_to_all(value, "row", 0, 0)


def in_hbm(value):
    return pltpu.with_memory_space_constraint(value, pltpu.HBM)


def flat(value):
    return value.reshape((-1,) + value.shape[2:])


def split(value, count):
    return value.reshape((count, -1) + value.shape[1:])


def per_device(inputs, teacher, gate_weight, up_weight, down_weight, block_mask):
    tokens, width = inputs.shape
    token_count = tokens * CHIPS * CORES
    units = gate_weight.shape[1]
    half = tokens * CHIPS
    scale = float(token_count) ** 0.5
    mask = jnp.transpose(block_mask, (0, 2, 1))
    slab = shaped((Z * tokens, width))
    piece = shaped((tokens, width))
    wide, tall = shaped((width, units)), shaped((units, width))
    gates, ups, downs, masks = (
        (value, other_core(value)) for value in (gate_weight, up_weight, down_weight, mask)
    )
    copies = jnp.broadcast_to(inputs[None], (CHIPS, tokens, width))
    chips = lax.all_to_all(copies, "col", 0, 0, axis_index_groups=SAME_CORE)
    *gate_ups, partial, rows = call(
        gate_up_kernel,
        (wide,) * 4 + (shaped((half, 4 * units)), shaped((half, width))),
        *masks,
        in_hbm(chips),
        *gates,
        in_hbm(ups[0]),
        ups[1],
        in_specs=[SMEM] * 2 + [ANY] + [VMEM] * 2 + [ANY, VMEM],
        scratch_shapes=[pltpu.VMEM(wide.shape, wide.dtype), pltpu.SemaphoreType.DMA((CHIPS + 1,))],
        flops=8 * half * width * units,
        vmem=16,
        after=downs[1:],
    )
    both, copies = call(
        hidden_kernel,
        (shaped((half // ROWS, 4 * units), jnp.float32), shaped((ROWS, half // ROWS, 2 * units))),
        exchange_row(split(partial, ROWS)),
    )
    hidden = flat(exchange_row(copies))
    *downs, first, second, third, fourth = multiply(
        output_kernel, (tall,) * 2 + (slab,) * X, [hidden], downs, masks
    )
    slabs = spread_x([first, second, third, fourth])
    parts = spread_z(call(sum_kernel, (piece,) * Z, *slabs))
    student, grad_out = call(functools.partial(error_kernel, scale), (piece, piece), teacher, *parts)
    slabs = gather_x(joined(gather_z(grad_out)))
    partial, grad_rows = multiply(
        grad_hidden_kernel, (shaped((half, 2 * units + BLK)), shaped((half, width))), slabs, downs
    )
    copies, squares = call(
        acts_kernel,
        (shaped((ROWS, half // ROWS, 4 * units)), DONE),
        exchange_row(split(partial, ROWS)),
        both,
    )
    acts = flat(exchange_row(copies))
    slabs = spread_x(multiply(grad_in_kernel, (slab,) * X, [acts], gate_ups))
    rows_other, hidden_other, grad_rows_other, acts_other, squares_other = (
        other_core(value) for value in (rows, hidden, grad_rows, acts, squares)
    )
    grad_gate, grad_up, grad_down, loss, done = call(
        weights_kernel,
        (wide, wide, tall, shaped((1, 1), jnp.float32), DONE),
        mask,
        rows,
        rows_other,
        acts,
        acts_other,
        hidden,
        hidden_other,
        grad_rows,
        grad_rows_other,
        squares,
        squares_other,
        in_specs=[SMEM] + [VMEM] * 10,
        out_specs=(ANY,) * 3 + (VMEM,) * 2,
        scratch_shapes=[pltpu.VMEM(value.shape, value.dtype) for value in (wide, wide, tall)]
        + [pltpu.SemaphoreType.DMA((6,))],
        flops=6 * token_count * width * units,
        vmem=24,
    )
    parts = spread_z(call(sum_kernel, (piece,) * Z, *slabs, after=(done,)))
    (grad_in,) = call(sum_kernel, (piece,), *parts)
    return student, loss[0, 0], grad_gate, grad_up, grad_down, grad_in


def solution(mesh):
    return jax.shard_map(
        per_device,
        mesh=mesh,
        in_specs=(
            P("col", "row"),
            P("col", "row"),
            P("row", "col"),
            P("row", "col"),
            P("col", "row"),
            P(None, "row", "col"),
        ),
        out_specs=(
            P("col", "row"),
            P(),
            P("row", "col"),
            P("row", "col"),
            P("col", "row"),
            P("col", "row"),
        ),
        check_vma=False,
    )
```

```python
import functools

import jax
import jax.numpy as jnp
from jax import lax
from jax.experimental import pallas as pl
from jax.experimental.pallas import tpu as pltpu
from jax.sharding import PartitionSpec as P

D = 8192
BLK = 128
X, Z, CORES = 4, 4, 2
CHIPS = X * Z
ROWS = 8
TILE = 512
DOWN = 2
SAME_CORE = [[chip * CORES + core for chip in range(CHIPS)] for core in range(CORES)]
VMEM = pl.BlockSpec(memory_space=pltpu.VMEM)
SMEM = pl.BlockSpec(memory_space=pltpu.SMEM)
ANY = pl.BlockSpec(memory_space=pl.ANY)


def call(kernel, shapes, *args, flops=0, vmem=12, in_specs=None, after=(), beside=False, **kwargs):
    moved = sum(a.size * a.dtype.itemsize for a in args)
    moved += sum(s.size * s.dtype.itemsize for s in jax.tree.leaves(shapes))
    return pl.pallas_call(
        lambda *refs: kernel(*refs[: len(args)], *refs[len(args) + len(after) :]),
        out_shape=shapes,
        in_specs=(in_specs or [VMEM] * len(args)) + [ANY] * len(after),
        compiler_params=pltpu.CompilerParams(vmem_limit_bytes=vmem << 20),
        cost_estimate=pl.CostEstimate(
            flops=0 if beside else flops, bytes_accessed=0 if beside else moved, transcendentals=0
        ),
        **kwargs,
    )(*args, *after)


def shaped(shape, dtype=jnp.bfloat16):
    return jax.ShapeDtypeStruct(shape, dtype)


DONE = shaped((8, BLK), jnp.float32)


def join_kernel(*refs):
    joined_ref = refs[-1]
    size = refs[0].shape[0]
    for part, ref in enumerate(refs[:-1]):
        joined_ref[pl.ds(part * size, size), :] = ref[...]


def keep(mask_ref, which, ref, kept_ref):
    for row in range(ref.shape[0] // BLK):
        for col in range(ref.shape[1] // BLK):
            at = (row, col) if which == DOWN else (col, row)
            factor = mask_ref[which, at[0], at[1]].astype(jnp.float32).astype(jnp.bfloat16)
            block = (pl.ds(row * BLK, BLK), pl.ds(col * BLK, BLK))
            kept_ref[block] = ref[block] * factor


def plain_dot(left, right):
    return jnp.dot(left, right, preferred_element_type=jnp.float32)


def other_turned_dot(left, right):
    return lax.dot_general(left, right, (((1,), (1,)), ((), ())), preferred_element_type=jnp.float32)


def gate_up_kernel(mask_ref, mask_other_ref, chips_ref, *refs):
    weights, kept_refs, (out_ref, rows_ref, scratch, sems) = list(refs[:4]), refs[4:8], refs[8:]
    chip = lax.axis_index("col") // CORES
    size = chips_ref.shape[1]
    pairs = [(weights[2], scratch)]
    for part in range(CHIPS):
        x = lax.rem(chip // Z + part // Z, X)
        z = lax.rem(chip + part % Z, Z)
        pairs.append((chips_ref.at[x * Z + z], rows_ref.at[pl.ds(part * size, size), :]))
    copies = [pltpu.make_async_copy(src, dst, sems.at[at]) for at, (src, dst) in enumerate(pairs)]
    for copy in copies[1:] + copies[:1]:
        copy.start()
    weights[2] = scratch

    def masked(which):
        keep((mask_ref, mask_other_ref)[which % 2], which // 2, weights[which], kept_refs[which])

    def multiplied(which):
        units = scratch.shape[1]
        value = plain_dot(rows_ref[...], kept_refs[which][...])
        out_ref[:, pl.ds(which * units, units)] = value.astype(out_ref.dtype)

    for which in (0, 1, 3):
        masked(which)
    for copy in copies[1:]:
        copy.wait()
    for which in (0, 1, 3):
        multiplied(which)
    copies[0].wait()
    masked(2)
    multiplied(2)


def put_slabs(out_refs, cols, value):
    size = out_refs[0].shape[0]
    for part, ref in enumerate(out_refs):
        ref[:, cols] = value[part * size : (part + 1) * size].astype(ref.dtype)


def output_kernel(mask_ref, mask_other_ref, hidden_ref, down_ref, down_other_ref, kept_ref, kept_other_ref, *out_refs):
    units, width = down_ref.shape
    keep(mask_ref, DOWN, down_ref, kept_ref)
    keep(mask_other_ref, DOWN, down_other_ref, kept_other_ref)
    for at in range(0, width, TILE):
        cols = pl.ds(at, TILE)
        value = plain_dot(hidden_ref[:, :units], kept_ref[:, cols])
        value = value + plain_dot(hidden_ref[:, units:], kept_other_ref[:, cols])
        put_slabs(out_refs, cols, value)


def grad_hidden_kernel(*refs):
    slabs, (down_ref, down_other_ref, out_ref, grad_ref) = refs[:X], refs[X:]
    join_kernel(*slabs, grad_ref)
    units = down_ref.shape[0]
    squares = jnp.sum(jnp.square(grad_ref[...].astype(jnp.float32)), axis=0, keepdims=True)
    squares = jnp.sum(squares, axis=1, keepdims=True)
    lane = lax.broadcasted_iota(jnp.int32, (out_ref.shape[0], BLK), 1)
    terms = jnp.zeros(lane.shape, jnp.float32)
    for which in range(3):
        term = squares.astype(jnp.bfloat16).astype(jnp.float32)
        terms = jnp.where(lane == which, term, terms)
        squares = squares - term
    out_ref[:, pl.ds(2 * units, BLK)] = terms.astype(out_ref.dtype)
    for which, ref in enumerate((down_ref, down_other_ref)):
        value = other_turned_dot(grad_ref[...], ref[...])
        out_ref[:, pl.ds(which * units, units)] = value.astype(out_ref.dtype)


def grad_in_kernel(acts_ref, *refs):
    weights, out_refs = refs[:-X], refs[-X:]
    width, units = weights[0].shape
    for at in range(0, width, TILE):
        value = None
        for which, ref in enumerate(weights):
            term = other_turned_dot(acts_ref[:, pl.ds(which * units, units)], ref[pl.ds(at, TILE), :])
            value = term if value is None else value + term
        put_slabs(out_refs, pl.ds(at, TILE), value)


def multiply(kernel, shapes, left, weights, masks=(), after=()):
    flops = 2 * sum(part.size // part.shape[-1] for part in left) * sum(weight.size for weight in weights)
    specs = [SMEM] * len(masks) + [VMEM] * (len(left) + len(weights))
    return call(kernel, shapes, *masks, *left, *weights, flops=flops, vmem=16, in_specs=specs, after=after)


def summed(parts):
    total = parts[0][...].astype(jnp.float32)
    for part in parts[1:]:
        total = total + part[...].astype(jnp.float32)
    return total


def parts_of(parts_ref):
    return [parts_ref.at[part] for part in range(parts_ref.shape[0])]


def hidden_kernel(parts_ref, both_ref, copies_ref):
    both = summed(parts_of(parts_ref))
    half = both.shape[1] // 2
    gate, up = both[:, :half], both[:, half:]
    hidden = (gate * jax.nn.sigmoid(gate) * up).astype(jnp.bfloat16)
    both_ref[...] = both
    for part in range(copies_ref.shape[0]):
        copies_ref[part] = hidden


def error_kernel(scale, teacher_ref, *refs):
    parts, (student_ref, grad_ref) = refs[:-2], refs[-2:]
    output = summed(parts)
    student_ref[...] = output.astype(jnp.bfloat16)
    grad_ref[...] = ((output - teacher_ref[...].astype(jnp.float32)) / scale).astype(jnp.bfloat16)


def acts_kernel(parts_ref, both_ref, copies_ref, squares_ref):
    total = summed(parts_of(parts_ref))
    half = both_ref.shape[1] // 2
    grad_hidden = total[:, :half]
    squares_ref[...] = jnp.broadcast_to(jnp.sum(total[:1, half:], axis=1, keepdims=True), squares_ref.shape)
    gate, up = both_ref[:, :half], both_ref[:, half:]
    sig = jax.nn.sigmoid(gate)
    grad_gate_act = (grad_hidden * up * sig * (1.0 + gate * (1.0 - sig))).astype(jnp.bfloat16)
    grad_up_act = (grad_hidden * (gate * sig)).astype(jnp.bfloat16)
    for part in range(copies_ref.shape[0]):
        copies_ref[part, :, :half] = grad_gate_act
        copies_ref[part, :, half:] = grad_up_act


def sum_kernel(*refs):
    parts, out_refs = refs[:X], refs[X:]
    put_slabs(out_refs, slice(None), summed(parts))


def put_kept(mask_ref, which, value, col, scratch_ref):
    for row in range(value.shape[0] // BLK):
        for step in range(value.shape[1] // BLK):
            at = (row, col + step) if which == DOWN else (col + step, row)
            factor = mask_ref[which, at[0], at[1]].astype(jnp.float32)
            block = value[row * BLK : (row + 1) * BLK, step * BLK : (step + 1) * BLK] * factor
            scratch_ref[pl.ds(row * BLK, BLK), pl.ds((col + step) * BLK, BLK)] = block.astype(jnp.bfloat16)


def weights_kernel(
    mask_ref,
    rows_ref,
    rows_other_ref,
    acts_ref,
    acts_other_ref,
    hidden_ref,
    hidden_other_ref,
    grad_ref,
    grad_other_ref,
    squares_ref,
    squares_other_ref,
    gate_ref,
    up_ref,
    down_ref,
    loss_ref,
    done_ref,
    gate_scratch,
    up_scratch,
    down_scratch,
    sems,
):
    units = gate_ref.shape[1]
    loss_ref[...] = (squares_ref[:1, :1] + squares_other_ref[:1, :1]) * (1.0 / D)
    done_ref[...] = jnp.zeros_like(done_ref)
    copies = []

    def put(which, value, col, scratch, out_ref):
        put_kept(mask_ref, which, value, col, scratch)
        cols = pl.ds(col * BLK, value.shape[1])
        copy = pltpu.make_async_copy(scratch.at[:, cols], out_ref.at[:, cols], sems.at[len(copies)])
        copy.start()
        copies.append(copy)

    turned, turned_other = hidden_ref[:, :units].T, hidden_other_ref[:, units:].T
    for col in range(0, down_ref.shape[1] // BLK, 4):
        cols = pl.ds(col * BLK, 4 * BLK)
        value = plain_dot(turned, grad_ref[:, cols]) + plain_dot(turned_other, grad_other_ref[:, cols])
        put(DOWN, value, col, down_scratch, down_ref)
    turned, turned_other = rows_ref[...].T, rows_other_ref[...].T
    for which, (scratch, out_ref) in enumerate(((gate_scratch, gate_ref), (up_scratch, up_ref))):
        for col in range(0, units // BLK, 2):
            own = pl.ds(2 * which * units + col * BLK, 2 * BLK)
            other = pl.ds((2 * which + 1) * units + col * BLK, 2 * BLK)
            value = plain_dot(turned, acts_ref[:, own]) + plain_dot(turned_other, acts_other_ref[:, other])
            put(which, value, col, scratch, out_ref)
    for copy in copies:
        copy.wait()


def hold_kernel(*refs):
    pass


def hold(values, after):
    return pl.pallas_call(
        hold_kernel,
        out_shape=[shaped(value.shape) for value in values],
        in_specs=[ANY] * (len(values) + len(after)),
        out_specs=[ANY] * len(values),
        input_output_aliases={at: at for at in range(len(values))},
        compiler_params=pltpu.CompilerParams(vmem_limit_bytes=1 << 20),
        cost_estimate=pl.CostEstimate(flops=0, bytes_accessed=0, transcendentals=0),
    )(*values, *after)


def other_core(value):
    count = CHIPS * CORES
    return lax.ppermute(value, "col", [(device, device ^ 1) for device in range(count)])


def fetch(value, dx, dz):
    pairs = [
        ((((x + dx) % X * Z + (z + dz) % Z) * CORES + core), (x * Z + z) * CORES + core)
        for x in range(X)
        for z in range(Z)
        for core in range(CORES)
    ]
    return lax.ppermute(value, "col", pairs)


def gather_z(block):
    return [block] + [fetch(block, 0, step) for step in range(1, Z)]


def joined(parts):
    size, width = parts[0].shape
    return call(join_kernel, shaped((len(parts) * size, width)), *parts)


def gather_x(block):
    return [block] + [fetch(block, step, 0) for step in range(1, X)]


def spread_x(parts):
    return [parts[0]] + [fetch(parts[step], -step, 0) for step in range(1, X)]


def spread_z(parts):
    return [parts[0]] + [fetch(parts[step], 0, -step) for step in range(1, Z)]


def exchange_row(value):
    return lax.all_to_all(value, "row", 0, 0)


def in_hbm(value):
    return pltpu.with_memory_space_constraint(value, pltpu.HBM)


def flat(value):
    return value.reshape((-1,) + value.shape[2:])


def split(value, count):
    return value.reshape((count, -1) + value.shape[1:])


def per_device(inputs, teacher, gate_weight, up_weight, down_weight, block_mask):
    tokens, width = inputs.shape
    token_count = tokens * CHIPS * CORES
    units = gate_weight.shape[1]
    half = tokens * CHIPS
    scale = float(token_count) ** 0.5
    mask = jnp.transpose(block_mask, (0, 2, 1))
    slab = shaped((Z * tokens, width))
    piece = shaped((tokens, width))
    wide, tall = shaped((width, units)), shaped((units, width))
    gates, ups, downs, masks = (
        (value, other_core(value)) for value in (gate_weight, up_weight, down_weight, mask)
    )
    copies = jnp.broadcast_to(inputs[None], (CHIPS, tokens, width))
    chips = lax.all_to_all(copies, "col", 0, 0, axis_index_groups=SAME_CORE)
    *gate_ups, partial, rows = call(
        gate_up_kernel,
        (wide,) * 4 + (shaped((half, 4 * units)), shaped((half, width))),
        *masks,
        in_hbm(chips),
        *gates,
        in_hbm(ups[0]),
        ups[1],
        in_specs=[SMEM] * 2 + [ANY] + [VMEM] * 2 + [ANY, VMEM],
        scratch_shapes=[pltpu.VMEM(wide.shape, wide.dtype), pltpu.SemaphoreType.DMA((CHIPS + 1,))],
        flops=8 * half * width * units,
        vmem=16,
        after=downs[1:],
    )
    both, copies = call(
        hidden_kernel,
        (shaped((half // ROWS, 4 * units), jnp.float32), shaped((ROWS, half // ROWS, 2 * units))),
        exchange_row(split(partial, ROWS)),
    )
    hidden = flat(exchange_row(copies))
    *downs, first, second, third, fourth = multiply(
        output_kernel, (tall,) * 2 + (slab,) * X, [hidden], downs, masks
    )
    slabs = spread_x([first, second, third, fourth])
    parts = call(sum_kernel, (piece,) * Z, *slabs)
    rows, hidden = hold((rows, hidden), parts[:1])
    rows_other, hidden_other = other_core(rows), other_core(hidden)
    parts = spread_z(parts)
    student, grad_out = call(functools.partial(error_kernel, scale), (piece, piece), teacher, *parts)
    slabs = gather_x(joined(gather_z(grad_out)))
    partial, grad_rows = multiply(
        grad_hidden_kernel, (shaped((half, 2 * units + BLK)), shaped((half, width))), slabs, downs, (), (rows_other, hidden_other)
    )
    copies, squares = call(
        acts_kernel,
        (shaped((ROWS, half // ROWS, 4 * units)), DONE),
        exchange_row(split(partial, ROWS)),
        both,
    )
    acts = flat(exchange_row(copies))
    slabs = spread_x(multiply(grad_in_kernel, (slab,) * X, [acts], gate_ups))
    grad_rows_other, acts_other, squares_other = (other_core(value) for value in (grad_rows, acts, squares))
    grad_gate, grad_up, grad_down, loss, done = call(
        weights_kernel,
        (wide, wide, tall, shaped((1, 1), jnp.float32), DONE),
        mask,
        rows,
        rows_other,
        acts,
        acts_other,
        hidden,
        hidden_other,
        grad_rows,
        grad_rows_other,
        squares,
        squares_other,
        in_specs=[SMEM] + [VMEM] * 10,
        out_specs=(ANY,) * 3 + (VMEM,) * 2,
        scratch_shapes=[pltpu.VMEM(value.shape, value.dtype) for value in (wide, wide, tall)]
        + [pltpu.SemaphoreType.DMA((6,))],
        flops=6 * token_count * width * units,
        vmem=24,
    )
    parts = spread_z(call(sum_kernel, (piece,) * Z, *slabs, after=(done,)))
    (grad_in,) = call(sum_kernel, (piece,), *parts)
    return student, loss[0, 0], grad_gate, grad_up, grad_down, grad_in


def solution(mesh):
    return jax.shard_map(
        per_device,
        mesh=mesh,
        in_specs=(
            P("col", "row"),
            P("col", "row"),
            P("row", "col"),
            P("row", "col"),
            P("col", "row"),
            P(None, "row", "col"),
        ),
        out_specs=(
            P("col", "row"),
            P(),
            P("row", "col"),
            P("row", "col"),
            P("col", "row"),
            P("col", "row"),
        ),
        check_vma=False,
    )
```

```python
import functools

import jax
import jax.numpy as jnp
from jax import lax
from jax.experimental import pallas as pl
from jax.experimental.pallas import tpu as pltpu
from jax.sharding import PartitionSpec as P

D = 8192
BLK = 128
X, Z, CORES = 4, 4, 2
CHIPS = X * Z
ROWS = 8
TILE = 512
DOWN = 2
PLACES = (0, 1, 3, 2)
SAME_CORE = [[chip * CORES + core for chip in range(CHIPS)] for core in range(CORES)]
VMEM = pl.BlockSpec(memory_space=pltpu.VMEM)
SMEM = pl.BlockSpec(memory_space=pltpu.SMEM)
ANY = pl.BlockSpec(memory_space=pl.ANY)


def call(kernel, shapes, *args, flops=0, vmem=12, in_specs=None, after=(), beside=False, **kwargs):
    moved = sum(a.size * a.dtype.itemsize for a in args)
    moved += sum(s.size * s.dtype.itemsize for s in jax.tree.leaves(shapes))
    return pl.pallas_call(
        lambda *refs: kernel(*refs[: len(args)], *refs[len(args) + len(after) :]),
        out_shape=shapes,
        in_specs=(in_specs or [VMEM] * len(args)) + [ANY] * len(after),
        compiler_params=pltpu.CompilerParams(vmem_limit_bytes=vmem << 20),
        cost_estimate=pl.CostEstimate(
            flops=0 if beside else flops, bytes_accessed=0 if beside else moved, transcendentals=0
        ),
        **kwargs,
    )(*args, *after)


def shaped(shape, dtype=jnp.bfloat16):
    return jax.ShapeDtypeStruct(shape, dtype)


DONE = shaped((8, BLK), jnp.float32)


def join_kernel(*refs):
    joined_ref = refs[-1]
    size = refs[0].shape[0]
    for place, ref in zip(PLACES, refs[:-1]):
        joined_ref[pl.ds(place * size, size), :] = ref[...]


def keep(mask_ref, which, ref, kept_ref):
    for row in range(ref.shape[0] // BLK):
        for col in range(ref.shape[1] // BLK):
            at = (row, col) if which == DOWN else (col, row)
            factor = mask_ref[which, at[0], at[1]].astype(jnp.float32).astype(jnp.bfloat16)
            block = (pl.ds(row * BLK, BLK), pl.ds(col * BLK, BLK))
            kept_ref[block] = ref[block] * factor


def plain_dot(left, right):
    return jnp.dot(left, right, preferred_element_type=jnp.float32)


def other_turned_dot(left, right):
    return lax.dot_general(left, right, (((1,), (1,)), ((), ())), preferred_element_type=jnp.float32)


def gate_up_kernel(mask_ref, mask_other_ref, chips_ref, *refs):
    weights, kept_refs, (out_ref, rows_ref, scratch, sems) = list(refs[:4]), refs[4:8], refs[8:]
    chip = lax.axis_index("col") // CORES
    size = chips_ref.shape[1]
    pairs = [(weights[2], scratch)]
    for part in range(CHIPS):
        x = lax.rem(chip // Z + part // Z, X)
        z = lax.rem(chip + part % Z, Z)
        pairs.append((chips_ref.at[x * Z + z], rows_ref.at[pl.ds(part * size, size), :]))
    copies = [pltpu.make_async_copy(src, dst, sems.at[at]) for at, (src, dst) in enumerate(pairs)]
    for copy in copies[1:] + copies[:1]:
        copy.start()
    weights[2] = scratch

    def masked(which):
        keep((mask_ref, mask_other_ref)[which % 2], which // 2, weights[which], kept_refs[which])

    def multiplied(which):
        units = scratch.shape[1]
        value = plain_dot(rows_ref[...], kept_refs[which][...])
        out_ref[:, pl.ds(which * units, units)] = value.astype(out_ref.dtype)

    for which in (0, 1, 3):
        masked(which)
    for copy in copies[1:]:
        copy.wait()
    for which in (0, 1, 3):
        multiplied(which)
    copies[0].wait()
    masked(2)
    multiplied(2)


def put_slabs(out_refs, cols, value):
    size = out_refs[0].shape[0]
    for part, ref in enumerate(out_refs):
        ref[:, cols] = value[part * size : (part + 1) * size].astype(ref.dtype)


def output_kernel(mask_ref, mask_other_ref, hidden_ref, down_ref, down_other_ref, kept_ref, kept_other_ref, *out_refs):
    units, width = down_ref.shape
    keep(mask_ref, DOWN, down_ref, kept_ref)
    keep(mask_other_ref, DOWN, down_other_ref, kept_other_ref)
    for at in range(0, width, TILE):
        cols = pl.ds(at, TILE)
        value = plain_dot(hidden_ref[:, :units], kept_ref[:, cols])
        value = value + plain_dot(hidden_ref[:, units:], kept_other_ref[:, cols])
        put_slabs(out_refs, cols, value)


def grad_hidden_kernel(*refs):
    slabs, (down_ref, down_other_ref, out_ref, grad_ref) = refs[:X], refs[X:]
    join_kernel(*slabs, grad_ref)
    units = down_ref.shape[0]
    squares = jnp.sum(jnp.square(grad_ref[...].astype(jnp.float32)), axis=0, keepdims=True)
    squares = jnp.sum(squares, axis=1, keepdims=True)
    lane = lax.broadcasted_iota(jnp.int32, (out_ref.shape[0], BLK), 1)
    terms = jnp.zeros(lane.shape, jnp.float32)
    for which in range(3):
        term = squares.astype(jnp.bfloat16).astype(jnp.float32)
        terms = jnp.where(lane == which, term, terms)
        squares = squares - term
    out_ref[:, pl.ds(2 * units, BLK)] = terms.astype(out_ref.dtype)
    for which, ref in enumerate((down_ref, down_other_ref)):
        value = other_turned_dot(grad_ref[...], ref[...])
        out_ref[:, pl.ds(which * units, units)] = value.astype(out_ref.dtype)


def grad_in_kernel(acts_ref, *refs):
    weights, out_refs = refs[:-X], refs[-X:]
    width, units = weights[0].shape
    for at in range(0, width, TILE):
        value = None
        for which, ref in enumerate(weights):
            term = other_turned_dot(acts_ref[:, pl.ds(which * units, units)], ref[pl.ds(at, TILE), :])
            value = term if value is None else value + term
        put_slabs(out_refs, pl.ds(at, TILE), value)


def multiply(kernel, shapes, left, weights, masks=(), after=()):
    flops = 2 * sum(part.size // part.shape[-1] for part in left) * sum(weight.size for weight in weights)
    specs = [SMEM] * len(masks) + [VMEM] * (len(left) + len(weights))
    return call(kernel, shapes, *masks, *left, *weights, flops=flops, vmem=16, in_specs=specs, after=after)


def summed(parts):
    total = parts[0][...].astype(jnp.float32)
    for part in parts[1:]:
        total = total + part[...].astype(jnp.float32)
    return total


def parts_of(parts_ref):
    return [parts_ref.at[part] for part in range(parts_ref.shape[0])]


def hidden_kernel(parts_ref, both_ref, copies_ref):
    both = summed(parts_of(parts_ref))
    half = both.shape[1] // 2
    gate, up = both[:, :half], both[:, half:]
    hidden = (gate * jax.nn.sigmoid(gate) * up).astype(jnp.bfloat16)
    both_ref[...] = both
    for part in range(copies_ref.shape[0]):
        copies_ref[part] = hidden


def error_kernel(scale, teacher_ref, *refs):
    parts, (student_ref, grad_ref) = refs[:-2], refs[-2:]
    output = summed(parts)
    student_ref[...] = output.astype(jnp.bfloat16)
    grad_ref[...] = ((output - teacher_ref[...].astype(jnp.float32)) / scale).astype(jnp.bfloat16)


def acts_kernel(parts_ref, both_ref, copies_ref, squares_ref):
    total = summed(parts_of(parts_ref))
    half = both_ref.shape[1] // 2
    grad_hidden = total[:, :half]
    squares_ref[...] = jnp.broadcast_to(jnp.sum(total[:1, half:], axis=1, keepdims=True), squares_ref.shape)
    gate, up = both_ref[:, :half], both_ref[:, half:]
    sig = jax.nn.sigmoid(gate)
    grad_gate_act = (grad_hidden * up * sig * (1.0 + gate * (1.0 - sig))).astype(jnp.bfloat16)
    grad_up_act = (grad_hidden * (gate * sig)).astype(jnp.bfloat16)
    for part in range(copies_ref.shape[0]):
        copies_ref[part, :, :half] = grad_gate_act
        copies_ref[part, :, half:] = grad_up_act


def sum_kernel(*refs):
    parts, out_refs = refs[:X], refs[X:]
    put_slabs(out_refs, slice(None), summed(parts))


def put_kept(mask_ref, which, value, col, scratch_ref):
    for row in range(value.shape[0] // BLK):
        for step in range(value.shape[1] // BLK):
            at = (row, col + step) if which == DOWN else (col + step, row)
            factor = mask_ref[which, at[0], at[1]].astype(jnp.float32)
            block = value[row * BLK : (row + 1) * BLK, step * BLK : (step + 1) * BLK] * factor
            scratch_ref[pl.ds(row * BLK, BLK), pl.ds((col + step) * BLK, BLK)] = block.astype(jnp.bfloat16)


def weights_kernel(
    mask_ref,
    rows_ref,
    rows_other_ref,
    acts_ref,
    acts_other_ref,
    hidden_ref,
    hidden_other_ref,
    grad_ref,
    grad_other_ref,
    squares_ref,
    squares_other_ref,
    gate_ref,
    up_ref,
    down_ref,
    loss_ref,
    done_ref,
    gate_scratch,
    up_scratch,
    down_scratch,
    sems,
):
    units = gate_ref.shape[1]
    loss_ref[...] = (squares_ref[:1, :1] + squares_other_ref[:1, :1]) * (1.0 / D)
    done_ref[...] = jnp.zeros_like(done_ref)
    copies = []

    def put(which, value, col, scratch, out_ref):
        put_kept(mask_ref, which, value, col, scratch)
        cols = pl.ds(col * BLK, value.shape[1])
        copy = pltpu.make_async_copy(scratch.at[:, cols], out_ref.at[:, cols], sems.at[len(copies)])
        copy.start()
        copies.append(copy)

    turned, turned_other = hidden_ref[:, :units].T, hidden_other_ref[:, units:].T
    for col in range(0, down_ref.shape[1] // BLK, 4):
        cols = pl.ds(col * BLK, 4 * BLK)
        value = plain_dot(turned, grad_ref[:, cols]) + plain_dot(turned_other, grad_other_ref[:, cols])
        put(DOWN, value, col, down_scratch, down_ref)
    turned, turned_other = rows_ref[...].T, rows_other_ref[...].T
    for which, (scratch, out_ref) in enumerate(((gate_scratch, gate_ref), (up_scratch, up_ref))):
        for col in range(0, units // BLK, 2):
            own = pl.ds(2 * which * units + col * BLK, 2 * BLK)
            other = pl.ds((2 * which + 1) * units + col * BLK, 2 * BLK)
            value = plain_dot(turned, acts_ref[:, own]) + plain_dot(turned_other, acts_other_ref[:, other])
            put(which, value, col, scratch, out_ref)
    for copy in copies:
        copy.wait()


def hold_kernel(*refs):
    pass


def hold(values, after):
    return pl.pallas_call(
        hold_kernel,
        out_shape=[shaped(value.shape) for value in values],
        in_specs=[ANY] * (len(values) + len(after)),
        out_specs=[ANY] * len(values),
        input_output_aliases={at: at for at in range(len(values))},
        compiler_params=pltpu.CompilerParams(vmem_limit_bytes=1 << 20),
        cost_estimate=pl.CostEstimate(flops=0, bytes_accessed=0, transcendentals=0),
    )(*values, *after)


def other_core(value):
    count = CHIPS * CORES
    return lax.ppermute(value, "col", [(device, device ^ 1) for device in range(count)])


def fetch(value, dx, dz):
    pairs = [
        ((((x + dx) % X * Z + (z + dz) % Z) * CORES + core), (x * Z + z) * CORES + core)
        for x in range(X)
        for z in range(Z)
        for core in range(CORES)
    ]
    return lax.ppermute(value, "col", pairs)


def gather_z(block):
    return [block] + [fetch(block, 0, step) for step in PLACES[1:]]


def joined(parts):
    size, width = parts[0].shape
    return call(join_kernel, shaped((len(parts) * size, width)), *parts)


def gather_x(block):
    return [block] + [fetch(block, step, 0) for step in PLACES[1:]]


def spread_x(parts):
    return [parts[0]] + [fetch(parts[step], -step, 0) for step in (2, 1, 3)]


def spread_z(parts):
    return [parts[0]] + [fetch(parts[step], 0, -step) for step in (2, 1, 3)]


def exchange_row(value):
    return lax.all_to_all(value, "row", 0, 0)


def in_hbm(value):
    return pltpu.with_memory_space_constraint(value, pltpu.HBM)


def flat(value):
    return value.reshape((-1,) + value.shape[2:])


def split(value, count):
    return value.reshape((count, -1) + value.shape[1:])


def per_device(inputs, teacher, gate_weight, up_weight, down_weight, block_mask):
    tokens, width = inputs.shape
    token_count = tokens * CHIPS * CORES
    units = gate_weight.shape[1]
    half = tokens * CHIPS
    scale = float(token_count) ** 0.5
    mask = jnp.transpose(block_mask, (0, 2, 1))
    slab = shaped((Z * tokens, width))
    piece = shaped((tokens, width))
    wide, tall = shaped((width, units)), shaped((units, width))
    gates, ups, downs, masks = (
        (value, other_core(value)) for value in (gate_weight, up_weight, down_weight, mask)
    )
    copies = jnp.broadcast_to(inputs[None], (CHIPS, tokens, width))
    chips = lax.all_to_all(copies, "col", 0, 0, axis_index_groups=SAME_CORE)
    *gate_ups, partial, rows = call(
        gate_up_kernel,
        (wide,) * 4 + (shaped((half, 4 * units)), shaped((half, width))),
        *masks,
        in_hbm(chips),
        *gates,
        in_hbm(ups[0]),
        ups[1],
        in_specs=[SMEM] * 2 + [ANY] + [VMEM] * 2 + [ANY, VMEM],
        scratch_shapes=[pltpu.VMEM(wide.shape, wide.dtype), pltpu.SemaphoreType.DMA((CHIPS + 1,))],
        flops=8 * half * width * units,
        vmem=16,
        after=downs[1:],
    )
    both, copies = call(
        hidden_kernel,
        (shaped((half // ROWS, 4 * units), jnp.float32), shaped((ROWS, half // ROWS, 2 * units))),
        exchange_row(split(partial, ROWS)),
    )
    hidden = flat(exchange_row(copies))
    *downs, first, second, third, fourth = multiply(
        output_kernel, (tall,) * 2 + (slab,) * X, [hidden], downs, masks
    )
    slabs = spread_x([first, second, third, fourth])
    parts = call(sum_kernel, (piece,) * Z, *slabs)
    rows, hidden = hold((rows, hidden), parts[:1])
    rows_other, hidden_other = other_core(rows), other_core(hidden)
    parts = spread_z(parts)
    student, grad_out = call(functools.partial(error_kernel, scale), (piece, piece), teacher, *parts)
    slabs = gather_x(joined(gather_z(grad_out)))
    partial, grad_rows = multiply(
        grad_hidden_kernel, (shaped((half, 2 * units + BLK)), shaped((half, width))), slabs, downs, (), (rows_other, hidden_other)
    )
    copies, squares = call(
        acts_kernel,
        (shaped((ROWS, half // ROWS, 4 * units)), DONE),
        exchange_row(split(partial, ROWS)),
        both,
    )
    acts = flat(exchange_row(copies))
    slabs = spread_x(multiply(grad_in_kernel, (slab,) * X, [acts], gate_ups))
    grad_rows_other, acts_other, squares_other = (other_core(value) for value in (grad_rows, acts, squares))
    grad_gate, grad_up, grad_down, loss, done = call(
        weights_kernel,
        (wide, wide, tall, shaped((1, 1), jnp.float32), DONE),
        mask,
        rows,
        rows_other,
        acts,
        acts_other,
        hidden,
        hidden_other,
        grad_rows,
        grad_rows_other,
        squares,
        squares_other,
        in_specs=[SMEM] + [VMEM] * 10,
        out_specs=(ANY,) * 3 + (VMEM,) * 2,
        scratch_shapes=[pltpu.VMEM(value.shape, value.dtype) for value in (wide, wide, tall)]
        + [pltpu.SemaphoreType.DMA((6,))],
        flops=6 * token_count * width * units,
        vmem=24,
    )
    parts = spread_z(call(sum_kernel, (piece,) * Z, *slabs, after=(done,)))
    (grad_in,) = call(sum_kernel, (piece,), *parts)
    return student, loss[0, 0], grad_gate, grad_up, grad_down, grad_in


def solution(mesh):
    return jax.shard_map(
        per_device,
        mesh=mesh,
        in_specs=(
            P("col", "row"),
            P("col", "row"),
            P("row", "col"),
            P("row", "col"),
            P("col", "row"),
            P(None, "row", "col"),
        ),
        out_specs=(
            P("col", "row"),
            P(),
            P("row", "col"),
            P("row", "col"),
            P("col", "row"),
            P("col", "row"),
        ),
        check_vma=False,
    )
```

```python
import functools

import jax
import jax.numpy as jnp
from jax import lax
from jax.experimental import pallas as pl
from jax.experimental.pallas import tpu as pltpu
from jax.sharding import PartitionSpec as P

D = 8192
BLK = 128
X, Z, CORES = 4, 4, 2
CHIPS = X * Z
ROWS = 8
TILE = 512
DOWN = 2
PLACES = (0, 1, 3, 2)
VMEM = pl.BlockSpec(memory_space=pltpu.VMEM)
SMEM = pl.BlockSpec(memory_space=pltpu.SMEM)
ANY = pl.BlockSpec(memory_space=pl.ANY)


def call(kernel, shapes, *args, flops=0, vmem=12, in_specs=None, after=(), beside=False, **kwargs):
    moved = sum(a.size * a.dtype.itemsize for a in args)
    moved += sum(s.size * s.dtype.itemsize for s in jax.tree.leaves(shapes))
    return pl.pallas_call(
        lambda *refs: kernel(*refs[: len(args)], *refs[len(args) + len(after) :]),
        out_shape=shapes,
        in_specs=(in_specs or [VMEM] * len(args)) + [ANY] * len(after),
        compiler_params=pltpu.CompilerParams(vmem_limit_bytes=vmem << 20),
        cost_estimate=pl.CostEstimate(
            flops=0 if beside else flops, bytes_accessed=0 if beside else moved, transcendentals=0
        ),
        **kwargs,
    )(*args, *after)


def shaped(shape, dtype=jnp.bfloat16):
    return jax.ShapeDtypeStruct(shape, dtype)


DONE = shaped((8, BLK), jnp.float32)


def join_kernel(*refs, places=PLACES):
    joined_ref = refs[-1]
    size = refs[0].shape[0]
    for place, ref in zip(places, refs[:-1]):
        joined_ref[pl.ds(place * size, size), :] = ref[...]


def keep(mask_ref, which, ref, kept_ref):
    for row in range(ref.shape[0] // BLK):
        for col in range(ref.shape[1] // BLK):
            at = (row, col) if which == DOWN else (col, row)
            factor = mask_ref[which, at[0], at[1]].astype(jnp.float32).astype(jnp.bfloat16)
            block = (pl.ds(row * BLK, BLK), pl.ds(col * BLK, BLK))
            kept_ref[block] = ref[block] * factor


def plain_dot(left, right):
    return jnp.dot(left, right, preferred_element_type=jnp.float32)


def other_turned_dot(left, right):
    return lax.dot_general(left, right, (((1,), (1,)), ((), ())), preferred_element_type=jnp.float32)


def gate_up_kernel(mask_ref, mask_other_ref, *refs):
    slabs, weights, kept_refs = refs[:X], list(refs[X : X + 4]), refs[X + 4 : X + 8]
    out_ref, rows_ref, scratch, sems = refs[X + 8 :]
    copies = {}
    for which in (0, 2):
        copies[which] = pltpu.make_async_copy(weights[which], scratch.at[which // 2], sems.at[which // 2])
        copies[which].start()
        weights[which] = scratch.at[which // 2]
    join_kernel(*slabs, rows_ref)
    for which in (1, 3, 0, 2):
        units = kept_refs[which].shape[1]
        if which in copies:
            copies[which].wait()
        keep((mask_ref, mask_other_ref)[which % 2], which // 2, weights[which], kept_refs[which])
        value = plain_dot(rows_ref[...], kept_refs[which][...])
        out_ref[:, pl.ds(which * units, units)] = value.astype(out_ref.dtype)


def keep_down_kernel(mask_ref, down_ref, kept_ref):
    keep(mask_ref, DOWN, down_ref, kept_ref)


def put_slabs(out_refs, cols, value):
    size = out_refs[0].shape[0]
    for part, ref in enumerate(out_refs):
        ref[:, cols] = value[part * size : (part + 1) * size].astype(ref.dtype)


def output_kernel(hidden_ref, down_ref, down_other_ref, *out_refs):
    units, width = down_ref.shape
    for at in range(0, width, TILE):
        cols = pl.ds(at, TILE)
        value = plain_dot(hidden_ref[:, :units], down_ref[:, cols])
        value = value + plain_dot(hidden_ref[:, units:], down_other_ref[:, cols])
        put_slabs(out_refs, cols, value)


def grad_hidden_kernel(*refs):
    slabs, (down_ref, down_other_ref, out_ref, grad_ref) = refs[:X], refs[X:]
    join_kernel(*slabs, grad_ref)
    units = down_ref.shape[0]
    squares = jnp.sum(jnp.square(grad_ref[...].astype(jnp.float32)), axis=0, keepdims=True)
    squares = jnp.sum(squares, axis=1, keepdims=True)
    lane = lax.broadcasted_iota(jnp.int32, (out_ref.shape[0], BLK), 1)
    terms = jnp.zeros(lane.shape, jnp.float32)
    for which in range(3):
        term = squares.astype(jnp.bfloat16).astype(jnp.float32)
        terms = jnp.where(lane == which, term, terms)
        squares = squares - term
    out_ref[:, pl.ds(2 * units, BLK)] = terms.astype(out_ref.dtype)
    for which, ref in enumerate((down_ref, down_other_ref)):
        value = other_turned_dot(grad_ref[...], ref[...])
        out_ref[:, pl.ds(which * units, units)] = value.astype(out_ref.dtype)


def grad_in_kernel(acts_ref, *refs):
    weights, out_refs = refs[:-X], refs[-X:]
    width, units = weights[0].shape
    for at in range(0, width, TILE):
        value = None
        for which, ref in enumerate(weights):
            term = other_turned_dot(acts_ref[:, pl.ds(which * units, units)], ref[pl.ds(at, TILE), :])
            value = term if value is None else value + term
        put_slabs(out_refs, pl.ds(at, TILE), value)


def multiply(kernel, shapes, left, weights, masks=(), after=()):
    flops = 2 * sum(part.size // part.shape[-1] for part in left) * sum(weight.size for weight in weights)
    specs = [SMEM] * len(masks) + [VMEM] * (len(left) + len(weights))
    return call(kernel, shapes, *masks, *left, *weights, flops=flops, vmem=16, in_specs=specs, after=after)


def summed(parts):
    total = parts[0][...].astype(jnp.float32)
    for part in parts[1:]:
        total = total + part[...].astype(jnp.float32)
    return total


def parts_of(parts_ref):
    return [parts_ref.at[part] for part in range(parts_ref.shape[0])]


def hidden_kernel(parts_ref, both_ref, copies_ref):
    both = summed(parts_of(parts_ref))
    half = both.shape[1] // 2
    gate, up = both[:, :half], both[:, half:]
    hidden = (gate * jax.nn.sigmoid(gate) * up).astype(jnp.bfloat16)
    both_ref[...] = both
    for part in range(copies_ref.shape[0]):
        copies_ref[part] = hidden


def error_kernel(scale, teacher_ref, *refs):
    parts, (student_ref, grad_ref) = refs[:-2], refs[-2:]
    output = summed(parts)
    student_ref[...] = output.astype(jnp.bfloat16)
    grad_ref[...] = ((output - teacher_ref[...].astype(jnp.float32)) / scale).astype(jnp.bfloat16)


def acts_kernel(parts_ref, both_ref, copies_ref, squares_ref):
    total = summed(parts_of(parts_ref))
    half = both_ref.shape[1] // 2
    grad_hidden = total[:, :half]
    squares_ref[...] = jnp.broadcast_to(jnp.sum(total[:1, half:], axis=1, keepdims=True), squares_ref.shape)
    gate, up = both_ref[:, :half], both_ref[:, half:]
    sig = jax.nn.sigmoid(gate)
    grad_gate_act = (grad_hidden * up * sig * (1.0 + gate * (1.0 - sig))).astype(jnp.bfloat16)
    grad_up_act = (grad_hidden * (gate * sig)).astype(jnp.bfloat16)
    for part in range(copies_ref.shape[0]):
        copies_ref[part, :, :half] = grad_gate_act
        copies_ref[part, :, half:] = grad_up_act


def sum_kernel(*refs):
    parts, out_refs = refs[:X], refs[X:]
    put_slabs(out_refs, slice(None), summed(parts))


def put_kept(mask_ref, which, value, col, scratch_ref):
    for row in range(value.shape[0] // BLK):
        for step in range(value.shape[1] // BLK):
            at = (row, col + step) if which == DOWN else (col + step, row)
            factor = mask_ref[which, at[0], at[1]].astype(jnp.float32)
            block = value[row * BLK : (row + 1) * BLK, step * BLK : (step + 1) * BLK] * factor
            scratch_ref[pl.ds(row * BLK, BLK), pl.ds((col + step) * BLK, BLK)] = block.astype(jnp.bfloat16)


def weights_kernel(
    mask_ref,
    rows_ref,
    rows_other_ref,
    acts_ref,
    acts_other_ref,
    hidden_ref,
    hidden_other_ref,
    grad_ref,
    grad_other_ref,
    squares_ref,
    squares_other_ref,
    gate_ref,
    up_ref,
    down_ref,
    loss_ref,
    done_ref,
    gate_scratch,
    up_scratch,
    down_scratch,
    sems,
):
    units = gate_ref.shape[1]
    loss_ref[...] = (squares_ref[:1, :1] + squares_other_ref[:1, :1]) * (1.0 / D)
    done_ref[...] = jnp.zeros_like(done_ref)
    copies = []

    def put(which, value, col, scratch, out_ref):
        put_kept(mask_ref, which, value, col, scratch)
        cols = pl.ds(col * BLK, value.shape[1])
        copy = pltpu.make_async_copy(scratch.at[:, cols], out_ref.at[:, cols], sems.at[len(copies)])
        copy.start()
        copies.append(copy)

    turned, turned_other = hidden_ref[:, :units].T, hidden_other_ref[:, units:].T
    for col in range(0, down_ref.shape[1] // BLK, 4):
        cols = pl.ds(col * BLK, 4 * BLK)
        value = plain_dot(turned, grad_ref[:, cols]) + plain_dot(turned_other, grad_other_ref[:, cols])
        put(DOWN, value, col, down_scratch, down_ref)
    turned, turned_other = rows_ref[...].T, rows_other_ref[...].T
    for which, (scratch, out_ref) in enumerate(((gate_scratch, gate_ref), (up_scratch, up_ref))):
        for col in range(0, units // BLK, 2):
            own = pl.ds(2 * which * units + col * BLK, 2 * BLK)
            other = pl.ds((2 * which + 1) * units + col * BLK, 2 * BLK)
            value = plain_dot(turned, acts_ref[:, own]) + plain_dot(turned_other, acts_other_ref[:, other])
            put(which, value, col, scratch, out_ref)
    for copy in copies:
        copy.wait()


def hold_kernel(*refs):
    pass


def hold(values, after):
    return pl.pallas_call(
        hold_kernel,
        out_shape=[shaped(value.shape) for value in values],
        in_specs=[ANY] * (len(values) + len(after)),
        out_specs=[ANY] * len(values),
        input_output_aliases={at: at for at in range(len(values))},
        compiler_params=pltpu.CompilerParams(vmem_limit_bytes=1 << 20),
        cost_estimate=pl.CostEstimate(flops=0, bytes_accessed=0, transcendentals=0),
    )(*values, *after)


def other_core(value):
    count = CHIPS * CORES
    return lax.ppermute(value, "col", [(device, device ^ 1) for device in range(count)])


def fetch(value, dx, dz):
    pairs = [
        ((((x + dx) % X * Z + (z + dz) % Z) * CORES + core), (x * Z + z) * CORES + core)
        for x in range(X)
        for z in range(Z)
        for core in range(CORES)
    ]
    return lax.ppermute(value, "col", pairs)


def gather_z(block, places=PLACES):
    return [block] + [fetch(block, 0, step) for step in places[1:]]


def joined(parts, places=PLACES, after=()):
    size, width = parts[0].shape
    kernel = functools.partial(join_kernel, places=places)
    return call(kernel, shaped((len(parts) * size, width)), *parts, after=after)


def gather_x(block):
    return [block] + [fetch(block, step, 0) for step in PLACES[1:]]


def spread_x(parts):
    return [parts[0]] + [fetch(parts[step], -step, 0) for step in (2, 1, 3)]


def spread_z(parts):
    return [parts[0]] + [fetch(parts[step], 0, -step) for step in (2, 1, 3)]


def exchange_row(value):
    return lax.all_to_all(value, "row", 0, 0)


def in_hbm(value):
    return pltpu.with_memory_space_constraint(value, pltpu.HBM)


def flat(value):
    return value.reshape((-1,) + value.shape[2:])


def split(value, count):
    return value.reshape((count, -1) + value.shape[1:])


def per_device(inputs, teacher, gate_weight, up_weight, down_weight, block_mask):
    tokens, width = inputs.shape
    token_count = tokens * CHIPS * CORES
    units = gate_weight.shape[1]
    half = tokens * CHIPS
    scale = float(token_count) ** 0.5
    mask = jnp.transpose(block_mask, (0, 2, 1))
    slab = shaped((Z * tokens, width))
    piece = shaped((tokens, width))
    wide, tall = shaped((width, units)), shaped((units, width))
    gates, ups, masks = ((value, other_core(value)) for value in (gate_weight, up_weight, mask))
    places = (0, 2, 1, 3)
    near = joined(gather_z(inputs, places), places, (gates[1], ups[1]))
    down = call(keep_down_kernel, tall, mask, down_weight, in_specs=[SMEM, VMEM], after=(near,))
    downs = (down, other_core(down))
    *gate_ups, partial, rows = call(
        gate_up_kernel,
        (wide,) * 4 + (shaped((half, 4 * units)), shaped((half, width))),
        *masks,
        *gather_x(near),
        in_hbm(gates[0]),
        gates[1],
        in_hbm(ups[0]),
        ups[1],
        in_specs=[SMEM] * 2 + [VMEM] * X + [ANY, VMEM] * 2,
        scratch_shapes=[pltpu.VMEM((2,) + wide.shape, wide.dtype), pltpu.SemaphoreType.DMA((2,))],
        flops=8 * half * width * units,
        vmem=16,
        after=downs[1:],
    )
    both, copies = call(
        hidden_kernel,
        (shaped((half // ROWS, 4 * units), jnp.float32), shaped((ROWS, half // ROWS, 2 * units))),
        exchange_row(split(partial, ROWS)),
    )
    hidden = flat(exchange_row(copies))
    slabs = spread_x(multiply(output_kernel, (slab,) * X, [hidden], downs))
    parts = call(sum_kernel, (piece,) * Z, *slabs)
    rows, hidden = hold((rows, hidden), parts[:1])
    rows_other, hidden_other = other_core(rows), other_core(hidden)
    parts = spread_z(parts)
    student, grad_out = call(functools.partial(error_kernel, scale), (piece, piece), teacher, *parts)
    slabs = gather_x(joined(gather_z(grad_out)))
    partial, grad_rows = multiply(
        grad_hidden_kernel, (shaped((half, 2 * units + BLK)), shaped((half, width))), slabs, downs, (), (rows_other, hidden_other)
    )
    copies, squares = call(
        acts_kernel,
        (shaped((ROWS, half // ROWS, 4 * units)), DONE),
        exchange_row(split(partial, ROWS)),
        both,
    )
    acts = flat(exchange_row(copies))
    slabs = spread_x(multiply(grad_in_kernel, (slab,) * X, [acts], gate_ups))
    grad_rows_other, acts_other, squares_other = (other_core(value) for value in (grad_rows, acts, squares))
    grad_gate, grad_up, grad_down, loss, done = call(
        weights_kernel,
        (wide, wide, tall, shaped((1, 1), jnp.float32), DONE),
        mask,
        rows,
        rows_other,
        acts,
        acts_other,
        hidden,
        hidden_other,
        grad_rows,
        grad_rows_other,
        squares,
        squares_other,
        in_specs=[SMEM] + [VMEM] * 10,
        out_specs=(ANY,) * 3 + (VMEM,) * 2,
        scratch_shapes=[pltpu.VMEM(value.shape, value.dtype) for value in (wide, wide, tall)]
        + [pltpu.SemaphoreType.DMA((6,))],
        flops=6 * token_count * width * units,
        vmem=24,
    )
    parts = spread_z(call(sum_kernel, (piece,) * Z, *slabs, after=(done,)))
    (grad_in,) = call(sum_kernel, (piece,), *parts)
    return student, loss[0, 0], grad_gate, grad_up, grad_down, grad_in


def solution(mesh):
    return jax.shard_map(
        per_device,
        mesh=mesh,
        in_specs=(
            P("col", "row"),
            P("col", "row"),
            P("row", "col"),
            P("row", "col"),
            P("col", "row"),
            P(None, "row", "col"),
        ),
        out_specs=(
            P("col", "row"),
            P(),
            P("row", "col"),
            P("row", "col"),
            P("col", "row"),
            P("col", "row"),
        ),
        check_vma=False,
    )
```

```python
import functools

import jax
import jax.numpy as jnp
from jax import lax
from jax.experimental import pallas as pl
from jax.experimental.pallas import tpu as pltpu
from jax.sharding import PartitionSpec as P

D = 8192
BLK = 128
X, Z, CORES = 4, 4, 2
CHIPS = X * Z
ROWS = 8
TILE = 512
DOWN = 2
PLACES = (0, 1, 3, 2)
VMEM = pl.BlockSpec(memory_space=pltpu.VMEM)
SMEM = pl.BlockSpec(memory_space=pltpu.SMEM)
ANY = pl.BlockSpec(memory_space=pl.ANY)


def call(kernel, shapes, *args, flops=0, vmem=12, in_specs=None, after=(), beside=False, **kwargs):
    moved = sum(a.size * a.dtype.itemsize for a in args)
    moved += sum(s.size * s.dtype.itemsize for s in jax.tree.leaves(shapes))
    return pl.pallas_call(
        lambda *refs: kernel(*refs[: len(args)], *refs[len(args) + len(after) :]),
        out_shape=shapes,
        in_specs=(in_specs or [VMEM] * len(args)) + [ANY] * len(after),
        compiler_params=pltpu.CompilerParams(vmem_limit_bytes=vmem << 20),
        cost_estimate=pl.CostEstimate(
            flops=0 if beside else flops, bytes_accessed=0 if beside else moved, transcendentals=0
        ),
        **kwargs,
    )(*args, *after)


def shaped(shape, dtype=jnp.bfloat16):
    return jax.ShapeDtypeStruct(shape, dtype)


DONE = shaped((8, BLK), jnp.float32)


def join_kernel(*refs, places=PLACES):
    joined_ref = refs[-1]
    size = refs[0].shape[0]
    for place, ref in zip(places, refs[:-1]):
        joined_ref[pl.ds(place * size, size), :] = ref[...]


def keep(mask_ref, which, ref, kept_ref):
    for row in range(ref.shape[0] // BLK):
        for col in range(ref.shape[1] // BLK):
            at = (row, col) if which == DOWN else (col, row)
            factor = mask_ref[which, at[0], at[1]].astype(jnp.float32).astype(jnp.bfloat16)
            block = (pl.ds(row * BLK, BLK), pl.ds(col * BLK, BLK))
            kept_ref[block] = ref[block] * factor


def plain_dot(left, right):
    return jnp.dot(left, right, preferred_element_type=jnp.float32)


def other_turned_dot(left, right):
    return lax.dot_general(left, right, (((1,), (1,)), ((), ())), preferred_element_type=jnp.float32)


def gate_up_kernel(mask_ref, mask_other_ref, *refs):
    slabs, weights, kept_refs = refs[:X], list(refs[X : X + 4]), refs[X + 4 : X + 8]
    out_ref, rows_ref, scratch, sems = refs[X + 8 :]
    copies = {}
    for which in (0, 2):
        copies[which] = pltpu.make_async_copy(weights[which], scratch.at[which // 2], sems.at[which // 2])
        copies[which].start()
        weights[which] = scratch.at[which // 2]
    join_kernel(*slabs, rows_ref)
    for which in (1, 3, 0, 2):
        units = kept_refs[which].shape[1]
        if which in copies:
            copies[which].wait()
        keep((mask_ref, mask_other_ref)[which % 2], which // 2, weights[which], kept_refs[which])
        value = plain_dot(rows_ref[...], kept_refs[which][...])
        out_ref[:, pl.ds(which * units, units)] = value.astype(out_ref.dtype)


def keep_down_kernel(mask_ref, down_ref, kept_ref):
    keep(mask_ref, DOWN, down_ref, kept_ref)


def put_slabs(out_refs, cols, value):
    size = out_refs[0].shape[0]
    for part, ref in enumerate(out_refs):
        ref[:, cols] = value[part * size : (part + 1) * size].astype(ref.dtype)


def output_kernel(hidden_ref, down_ref, down_other_ref, *out_refs):
    units, width = down_ref.shape
    for at in range(0, width, TILE):
        cols = pl.ds(at, TILE)
        value = plain_dot(hidden_ref[:, :units], down_ref[:, cols])
        value = value + plain_dot(hidden_ref[:, units:], down_other_ref[:, cols])
        put_slabs(out_refs, cols, value)


def grad_hidden_kernel(*refs):
    slabs, (down_ref, down_other_ref, out_ref, grad_ref) = refs[:X], refs[X:]
    join_kernel(*slabs, grad_ref)
    units = down_ref.shape[0]
    squares = jnp.sum(jnp.square(grad_ref[...].astype(jnp.float32)), axis=0, keepdims=True)
    squares = jnp.sum(squares, axis=1, keepdims=True)
    lane = lax.broadcasted_iota(jnp.int32, (out_ref.shape[0], BLK), 1)
    terms = jnp.zeros(lane.shape, jnp.float32)
    for which in range(3):
        term = squares.astype(jnp.bfloat16).astype(jnp.float32)
        terms = jnp.where(lane == which, term, terms)
        squares = squares - term
    out_ref[:, pl.ds(2 * units, BLK)] = terms.astype(out_ref.dtype)
    for which, ref in enumerate((down_ref, down_other_ref)):
        value = other_turned_dot(grad_ref[...], ref[...])
        out_ref[:, pl.ds(which * units, units)] = value.astype(out_ref.dtype)


def grad_in_kernel(acts_ref, *refs):
    weights, out_refs = refs[:-X], refs[-X:]
    width, units = weights[0].shape
    for at in range(0, width, TILE):
        value = None
        for which, ref in enumerate(weights):
            term = other_turned_dot(acts_ref[:, pl.ds(which * units, units)], ref[pl.ds(at, TILE), :])
            value = term if value is None else value + term
        put_slabs(out_refs, pl.ds(at, TILE), value)


def multiply(kernel, shapes, left, weights, masks=(), after=()):
    flops = 2 * sum(part.size // part.shape[-1] for part in left) * sum(weight.size for weight in weights)
    specs = [SMEM] * len(masks) + [VMEM] * (len(left) + len(weights))
    return call(kernel, shapes, *masks, *left, *weights, flops=flops, vmem=16, in_specs=specs, after=after)


def summed(parts):
    total = parts[0][...].astype(jnp.float32)
    for part in parts[1:]:
        total = total + part[...].astype(jnp.float32)
    return total


def parts_of(parts_ref):
    return [parts_ref.at[part] for part in range(parts_ref.shape[0])]


def hidden_kernel(parts_ref, both_ref, copies_ref):
    both = summed(parts_of(parts_ref))
    half = both.shape[1] // 2
    gate, up = both[:, :half], both[:, half:]
    hidden = (gate * jax.nn.sigmoid(gate) * up).astype(jnp.bfloat16)
    both_ref[...] = both
    for part in range(copies_ref.shape[0]):
        copies_ref[part] = hidden


def error_kernel(scale, teacher_ref, *refs):
    parts, (student_ref, grad_ref) = refs[:-2], refs[-2:]
    output = summed(parts)
    student_ref[...] = output.astype(jnp.bfloat16)
    grad_ref[...] = ((output - teacher_ref[...].astype(jnp.float32)) / scale).astype(jnp.bfloat16)


def acts_kernel(parts_ref, both_ref, copies_ref, squares_ref):
    total = summed(parts_of(parts_ref))
    half = both_ref.shape[1] // 2
    grad_hidden = total[:, :half]
    squares_ref[...] = jnp.broadcast_to(jnp.sum(total[:1, half:], axis=1, keepdims=True), squares_ref.shape)
    gate, up = both_ref[:, :half], both_ref[:, half:]
    sig = jax.nn.sigmoid(gate)
    grad_gate_act = (grad_hidden * up * sig * (1.0 + gate * (1.0 - sig))).astype(jnp.bfloat16)
    grad_up_act = (grad_hidden * (gate * sig)).astype(jnp.bfloat16)
    for part in range(copies_ref.shape[0]):
        copies_ref[part, :, :half] = grad_gate_act
        copies_ref[part, :, half:] = grad_up_act


def sum_kernel(*refs):
    parts, out_refs = refs[:X], refs[X:]
    put_slabs(out_refs, slice(None), summed(parts))


def put_kept(mask_ref, which, value, col, scratch_ref):
    for row in range(value.shape[0] // BLK):
        for step in range(value.shape[1] // BLK):
            at = (row, col + step) if which == DOWN else (col + step, row)
            factor = mask_ref[which, at[0], at[1]].astype(jnp.float32)
            block = value[row * BLK : (row + 1) * BLK, step * BLK : (step + 1) * BLK] * factor
            scratch_ref[pl.ds(row * BLK, BLK), pl.ds((col + step) * BLK, BLK)] = block.astype(jnp.bfloat16)


def weights_kernel(
    mask_ref,
    rows_ref,
    rows_other_ref,
    acts_ref,
    acts_other_ref,
    hidden_ref,
    hidden_other_ref,
    grad_ref,
    grad_other_ref,
    squares_ref,
    squares_other_ref,
    gate_ref,
    up_ref,
    down_ref,
    loss_ref,
    done_ref,
    gate_scratch,
    up_scratch,
    down_scratch,
    sems,
):
    units = gate_ref.shape[1]
    loss_ref[...] = (squares_ref[:1, :1] + squares_other_ref[:1, :1]) * (1.0 / D)
    done_ref[...] = jnp.zeros_like(done_ref)
    copies = []

    def put(which, value, col, scratch, out_ref):
        put_kept(mask_ref, which, value, col, scratch)
        cols = pl.ds(col * BLK, value.shape[1])
        copy = pltpu.make_async_copy(scratch.at[:, cols], out_ref.at[:, cols], sems.at[len(copies)])
        copy.start()
        copies.append(copy)

    turned, turned_other = hidden_ref[:, :units].T, hidden_other_ref[:, units:].T
    for col in range(0, down_ref.shape[1] // BLK, 4):
        cols = pl.ds(col * BLK, 4 * BLK)
        value = plain_dot(turned, grad_ref[:, cols]) + plain_dot(turned_other, grad_other_ref[:, cols])
        put(DOWN, value, col, down_scratch, down_ref)
    turned, turned_other = rows_ref[...].T, rows_other_ref[...].T
    for which, (scratch, out_ref) in enumerate(((gate_scratch, gate_ref), (up_scratch, up_ref))):
        for col in range(0, units // BLK, 2):
            own = pl.ds(2 * which * units + col * BLK, 2 * BLK)
            other = pl.ds((2 * which + 1) * units + col * BLK, 2 * BLK)
            value = plain_dot(turned, acts_ref[:, own]) + plain_dot(turned_other, acts_other_ref[:, other])
            put(which, value, col, scratch, out_ref)
    for copy in copies:
        copy.wait()


def hold_kernel(*refs):
    pass


def hold(values, after):
    return pl.pallas_call(
        hold_kernel,
        out_shape=[shaped(value.shape) for value in values],
        in_specs=[ANY] * (len(values) + len(after)),
        out_specs=[ANY] * len(values),
        input_output_aliases={at: at for at in range(len(values))},
        compiler_params=pltpu.CompilerParams(vmem_limit_bytes=1 << 20),
        cost_estimate=pl.CostEstimate(flops=0, bytes_accessed=0, transcendentals=0),
    )(*values, *after)


def other_core(value):
    count = CHIPS * CORES
    return lax.ppermute(value, "col", [(device, device ^ 1) for device in range(count)])


def fetch(value, dx, dz):
    pairs = [
        ((((x + dx) % X * Z + (z + dz) % Z) * CORES + core), (x * Z + z) * CORES + core)
        for x in range(X)
        for z in range(Z)
        for core in range(CORES)
    ]
    return lax.ppermute(value, "col", pairs)


def gather_z(block, places=PLACES):
    return [block] + [fetch(block, 0, step) for step in places[1:]]


def joined(parts, places=PLACES, after=()):
    size, width = parts[0].shape
    kernel = functools.partial(join_kernel, places=places)
    return call(kernel, shaped((len(parts) * size, width)), *parts, after=after)


def gather_x(block):
    return [block] + [fetch(block, step, 0) for step in PLACES[1:]]


def spread_x(parts):
    return [parts[0]] + [fetch(parts[step], -step, 0) for step in (2, 1, 3)]


def spread_z(parts):
    return [parts[0]] + [fetch(parts[step], 0, -step) for step in (2, 1, 3)]


def exchange_row(value):
    return lax.all_to_all(value, "row", 0, 0)


def in_hbm(value):
    return pltpu.with_memory_space_constraint(value, pltpu.HBM)


def flat(value):
    return value.reshape((-1,) + value.shape[2:])


def split(value, count):
    return value.reshape((count, -1) + value.shape[1:])


def per_device(inputs, teacher, gate_weight, up_weight, down_weight, block_mask):
    tokens, width = inputs.shape
    token_count = tokens * CHIPS * CORES
    units = gate_weight.shape[1]
    half = tokens * CHIPS
    scale = float(token_count) ** 0.5
    mask = jnp.transpose(block_mask, (0, 2, 1))
    slab = shaped((Z * tokens, width))
    piece = shaped((tokens, width))
    wide, tall = shaped((width, units)), shaped((units, width))
    gates, ups, masks = ((value, other_core(value)) for value in (gate_weight, up_weight, mask))
    places = (0, 2, 1, 3)
    near = joined(gather_z(inputs, places), places, (gates[1], ups[1]))
    down = call(keep_down_kernel, tall, mask, down_weight, in_specs=[SMEM, VMEM], after=(near,))
    downs = (down, other_core(down))
    *gate_ups, partial, rows = call(
        gate_up_kernel,
        (wide,) * 4 + (shaped((half, 4 * units)), shaped((half, width))),
        *masks,
        *gather_x(near),
        in_hbm(gates[0]),
        gates[1],
        in_hbm(ups[0]),
        ups[1],
        in_specs=[SMEM] * 2 + [VMEM] * X + [ANY, VMEM] * 2,
        scratch_shapes=[pltpu.VMEM((2,) + wide.shape, wide.dtype), pltpu.SemaphoreType.DMA((2,))],
        flops=8 * half * width * units,
        vmem=16,
        after=downs[1:],
    )
    both, copies = call(
        hidden_kernel,
        (shaped((half // ROWS, 4 * units), jnp.float32), shaped((ROWS, half // ROWS, 2 * units))),
        exchange_row(split(partial, ROWS)),
    )
    hidden = flat(exchange_row(copies))
    slabs = spread_x(multiply(output_kernel, (slab,) * X, [hidden], downs))
    parts = call(sum_kernel, (piece,) * Z, *slabs)
    rows, hidden = hold((rows, hidden), parts[:1])
    rows_other, hidden_other = other_core(rows), other_core(hidden)
    parts = spread_z(parts)
    student, grad_out = call(functools.partial(error_kernel, scale), (piece, piece), teacher, *parts)
    slabs = gather_x(joined(gather_z(grad_out)))
    partial, grad_rows = multiply(
        grad_hidden_kernel, (shaped((half, 2 * units + BLK)), shaped((half, width))), slabs, downs, (), (rows_other, hidden_other)
    )
    copies, squares = call(
        acts_kernel,
        (shaped((ROWS, half // ROWS, 4 * units)), DONE),
        exchange_row(split(partial, ROWS)),
        both,
    )
    acts = flat(exchange_row(copies))
    slabs = spread_x(multiply(grad_in_kernel, (slab,) * X, [acts], gate_ups))
    grad_rows_other, acts_other, squares_other = (other_core(value) for value in (grad_rows, acts, squares))
    grad_gate, grad_up, grad_down, loss, done = call(
        weights_kernel,
        (wide, wide, tall, shaped((1, 1), jnp.float32), DONE),
        mask,
        rows,
        rows_other,
        acts,
        acts_other,
        hidden,
        hidden_other,
        grad_rows,
        grad_rows_other,
        squares,
        squares_other,
        in_specs=[SMEM] + [VMEM] * 10,
        out_specs=(ANY,) * 3 + (VMEM,) * 2,
        scratch_shapes=[pltpu.VMEM(value.shape, value.dtype) for value in (wide, wide, tall)]
        + [pltpu.SemaphoreType.DMA((6,))],
        flops=6 * token_count * width * units,
        vmem=24,
    )
    parts = spread_z(call(sum_kernel, (piece,) * Z, *slabs))
    (grad_in,) = call(sum_kernel, (piece,), *parts, after=(done,))
    return student, loss[0, 0], grad_gate, grad_up, grad_down, grad_in


def solution(mesh):
    return jax.shard_map(
        per_device,
        mesh=mesh,
        in_specs=(
            P("col", "row"),
            P("col", "row"),
            P("row", "col"),
            P("row", "col"),
            P("col", "row"),
            P(None, "row", "col"),
        ),
        out_specs=(
            P("col", "row"),
            P(),
            P("row", "col"),
            P("row", "col"),
            P("col", "row"),
            P("col", "row"),
        ),
        check_vma=False,
    )
```

```python
import functools

import jax
import jax.numpy as jnp
from jax import lax
from jax.experimental import pallas as pl
from jax.experimental.pallas import tpu as pltpu
from jax.sharding import PartitionSpec as P

D = 8192
BLK = 128
X, Z, CORES = 4, 4, 2
CHIPS = X * Z
ROWS = 8
TILE = 512
DOWN = 2
PLACES = (0, 1, 3, 2)
VMEM = pl.BlockSpec(memory_space=pltpu.VMEM)
SMEM = pl.BlockSpec(memory_space=pltpu.SMEM)
ANY = pl.BlockSpec(memory_space=pl.ANY)


def call(kernel, shapes, *args, flops=0, vmem=12, in_specs=None, after=(), beside=False, **kwargs):
    moved = sum(a.size * a.dtype.itemsize for a in args)
    moved += sum(s.size * s.dtype.itemsize for s in jax.tree.leaves(shapes))
    return pl.pallas_call(
        lambda *refs: kernel(*refs[: len(args)], *refs[len(args) + len(after) :]),
        out_shape=shapes,
        in_specs=(in_specs or [VMEM] * len(args)) + [ANY] * len(after),
        compiler_params=pltpu.CompilerParams(vmem_limit_bytes=vmem << 20),
        cost_estimate=pl.CostEstimate(
            flops=0 if beside else flops, bytes_accessed=0 if beside else moved, transcendentals=0
        ),
        **kwargs,
    )(*args, *after)


def shaped(shape, dtype=jnp.bfloat16):
    return jax.ShapeDtypeStruct(shape, dtype)


DONE = shaped((8, BLK), jnp.float32)


def join_kernel(*refs, places=PLACES):
    joined_ref = refs[-1]
    size = refs[0].shape[0]
    for place, ref in zip(places, refs[:-1]):
        joined_ref[pl.ds(place * size, size), :] = ref[...]


def keep(mask_ref, which, ref, kept_ref):
    for row in range(ref.shape[0] // BLK):
        for col in range(ref.shape[1] // BLK):
            at = (row, col) if which == DOWN else (col, row)
            factor = mask_ref[which, at[0], at[1]].astype(jnp.float32).astype(jnp.bfloat16)
            block = (pl.ds(row * BLK, BLK), pl.ds(col * BLK, BLK))
            kept_ref[block] = ref[block] * factor


def plain_dot(left, right):
    return jnp.dot(left, right, preferred_element_type=jnp.float32)


def other_turned_dot(left, right):
    return lax.dot_general(left, right, (((1,), (1,)), ((), ())), preferred_element_type=jnp.float32)


def gate_up_kernel(mask_ref, mask_other_ref, *refs):
    slabs, weights, kept_refs = refs[:X], list(refs[X : X + 4]), refs[X + 4 : X + 8]
    out_ref, rows_ref, scratch, sems = refs[X + 8 :]
    copies = {}
    for which in (0, 2):
        copies[which] = pltpu.make_async_copy(weights[which], scratch.at[which // 2], sems.at[which // 2])
        copies[which].start()
        weights[which] = scratch.at[which // 2]
    join_kernel(*slabs, rows_ref)
    for which in (1, 3, 0, 2):
        units = kept_refs[which].shape[1]
        if which in copies:
            copies[which].wait()
        keep((mask_ref, mask_other_ref)[which % 2], which // 2, weights[which], kept_refs[which])
        value = plain_dot(rows_ref[...], kept_refs[which][...])
        out_ref[:, pl.ds(which * units, units)] = value.astype(out_ref.dtype)


def keep_down_kernel(mask_ref, down_ref, kept_ref):
    keep(mask_ref, DOWN, down_ref, kept_ref)


def put_slabs(out_refs, cols, value):
    size = out_refs[0].shape[0]
    for part, ref in enumerate(out_refs):
        ref[:, cols] = value[part * size : (part + 1) * size].astype(ref.dtype)


def output_kernel(hidden_ref, down_ref, down_other_ref, *out_refs):
    units, width = down_ref.shape
    for at in range(0, width, TILE):
        cols = pl.ds(at, TILE)
        value = plain_dot(hidden_ref[:, :units], down_ref[:, cols])
        value = value + plain_dot(hidden_ref[:, units:], down_other_ref[:, cols])
        put_slabs(out_refs, cols, value)


def grad_hidden_kernel(*refs):
    slabs, (down_ref, down_other_ref, out_ref, grad_ref) = refs[:X], refs[X:]
    join_kernel(*slabs, grad_ref)
    units = down_ref.shape[0]
    squares = jnp.sum(jnp.square(grad_ref[...].astype(jnp.float32)), axis=0, keepdims=True)
    squares = jnp.sum(squares, axis=1, keepdims=True)
    lane = lax.broadcasted_iota(jnp.int32, (out_ref.shape[0], BLK), 1)
    terms = jnp.zeros(lane.shape, jnp.float32)
    for which in range(3):
        term = squares.astype(jnp.bfloat16).astype(jnp.float32)
        terms = jnp.where(lane == which, term, terms)
        squares = squares - term
    out_ref[:, pl.ds(2 * units, BLK)] = terms.astype(out_ref.dtype)
    for which, ref in enumerate((down_ref, down_other_ref)):
        value = other_turned_dot(grad_ref[...], ref[...])
        out_ref[:, pl.ds(which * units, units)] = value.astype(out_ref.dtype)


def grad_in_kernel(acts_ref, *refs):
    weights, out_refs = refs[:-X], refs[-X:]
    width, units = weights[0].shape
    for at in range(0, width, TILE):
        value = None
        for which, ref in enumerate(weights):
            term = other_turned_dot(acts_ref[:, pl.ds(which * units, units)], ref[pl.ds(at, TILE), :])
            value = term if value is None else value + term
        put_slabs(out_refs, pl.ds(at, TILE), value)


def multiply(kernel, shapes, left, weights, masks=(), after=()):
    flops = 2 * sum(part.size // part.shape[-1] for part in left) * sum(weight.size for weight in weights)
    specs = [SMEM] * len(masks) + [VMEM] * (len(left) + len(weights))
    return call(kernel, shapes, *masks, *left, *weights, flops=flops, vmem=16, in_specs=specs, after=after)


def summed(parts):
    total = parts[0][...].astype(jnp.float32)
    for part in parts[1:]:
        total = total + part[...].astype(jnp.float32)
    return total


def parts_of(parts_ref):
    return [parts_ref.at[part] for part in range(parts_ref.shape[0])]


def hidden_kernel(parts_ref, both_ref, copies_ref):
    both = summed(parts_of(parts_ref))
    half = both.shape[1] // 2
    gate, up = both[:, :half], both[:, half:]
    hidden = (gate * jax.nn.sigmoid(gate) * up).astype(jnp.bfloat16)
    both_ref[...] = both
    for part in range(copies_ref.shape[0]):
        copies_ref[part] = hidden


def error_kernel(scale, teacher_ref, *refs):
    parts, (student_ref, grad_ref) = refs[:-2], refs[-2:]
    output = summed(parts)
    student_ref[...] = output.astype(jnp.bfloat16)
    grad_ref[...] = ((output - teacher_ref[...].astype(jnp.float32)) / scale).astype(jnp.bfloat16)


def acts_kernel(parts_ref, both_ref, copies_ref, squares_ref):
    total = summed(parts_of(parts_ref))
    half = both_ref.shape[1] // 2
    grad_hidden = total[:, :half]
    squares_ref[...] = jnp.broadcast_to(jnp.sum(total[:1, half:], axis=1, keepdims=True), squares_ref.shape)
    gate, up = both_ref[:, :half], both_ref[:, half:]
    sig = jax.nn.sigmoid(gate)
    grad_gate_act = (grad_hidden * up * sig * (1.0 + gate * (1.0 - sig))).astype(jnp.bfloat16)
    grad_up_act = (grad_hidden * (gate * sig)).astype(jnp.bfloat16)
    for part in range(copies_ref.shape[0]):
        copies_ref[part, :, :half] = grad_gate_act
        copies_ref[part, :, half:] = grad_up_act


def sum_kernel(*refs):
    parts, out_refs = refs[:X], refs[X:]
    put_slabs(out_refs, slice(None), summed(parts))


def put_kept(mask_ref, which, value, col, scratch_ref):
    for row in range(value.shape[0] // BLK):
        for step in range(value.shape[1] // BLK):
            at = (row, col + step) if which == DOWN else (col + step, row)
            factor = mask_ref[which, at[0], at[1]].astype(jnp.float32)
            block = value[row * BLK : (row + 1) * BLK, step * BLK : (step + 1) * BLK] * factor
            scratch_ref[pl.ds(row * BLK, BLK), pl.ds((col + step) * BLK, BLK)] = block.astype(jnp.bfloat16)


def weights_kernel(
    mask_ref,
    rows_ref,
    rows_other_ref,
    acts_ref,
    acts_other_ref,
    hidden_ref,
    hidden_other_ref,
    grad_ref,
    grad_other_ref,
    squares_ref,
    squares_other_ref,
    gate_ref,
    up_ref,
    down_ref,
    loss_ref,
    done_ref,
    gate_scratch,
    up_scratch,
    down_scratch,
    sems,
):
    units = gate_ref.shape[1]
    loss_ref[...] = (squares_ref[:1, :1] + squares_other_ref[:1, :1]) * (1.0 / D)
    done_ref[...] = jnp.zeros_like(done_ref)
    copies = []

    def put(which, value, col, scratch, out_ref):
        put_kept(mask_ref, which, value, col, scratch)
        cols = pl.ds(col * BLK, value.shape[1])
        copy = pltpu.make_async_copy(scratch.at[:, cols], out_ref.at[:, cols], sems.at[len(copies)])
        copy.start()
        copies.append(copy)

    turned, turned_other = hidden_ref[:, :units].T, hidden_other_ref[:, units:].T
    for col in range(0, down_ref.shape[1] // BLK, 4):
        cols = pl.ds(col * BLK, 4 * BLK)
        value = plain_dot(turned, grad_ref[:, cols]) + plain_dot(turned_other, grad_other_ref[:, cols])
        put(DOWN, value, col, down_scratch, down_ref)
    turned, turned_other = rows_ref[...].T, rows_other_ref[...].T
    for which, (scratch, out_ref) in enumerate(((gate_scratch, gate_ref), (up_scratch, up_ref))):
        for col in range(0, units // BLK, 2):
            own = pl.ds(2 * which * units + col * BLK, 2 * BLK)
            other = pl.ds((2 * which + 1) * units + col * BLK, 2 * BLK)
            value = plain_dot(turned, acts_ref[:, own]) + plain_dot(turned_other, acts_other_ref[:, other])
            put(which, value, col, scratch, out_ref)
    for copy in copies:
        copy.wait()


def hold_kernel(*refs):
    pass


def hold(values, after):
    return pl.pallas_call(
        hold_kernel,
        out_shape=[shaped(value.shape) for value in values],
        in_specs=[ANY] * (len(values) + len(after)),
        out_specs=[ANY] * len(values),
        input_output_aliases={at: at for at in range(len(values))},
        compiler_params=pltpu.CompilerParams(vmem_limit_bytes=1 << 20),
        cost_estimate=pl.CostEstimate(flops=0, bytes_accessed=0, transcendentals=0),
    )(*values, *after)


def other_core(value):
    count = CHIPS * CORES
    return lax.ppermute(value, "col", [(device, device ^ 1) for device in range(count)])


def fetch(value, dx, dz):
    pairs = [
        ((((x + dx) % X * Z + (z + dz) % Z) * CORES + core), (x * Z + z) * CORES + core)
        for x in range(X)
        for z in range(Z)
        for core in range(CORES)
    ]
    return lax.ppermute(value, "col", pairs)


def gather_z(block, places=PLACES):
    return [block] + [fetch(block, 0, step) for step in places[1:]]


def joined(parts, places=PLACES, after=()):
    size, width = parts[0].shape
    kernel = functools.partial(join_kernel, places=places)
    return call(kernel, shaped((len(parts) * size, width)), *parts, after=after)


def gather_x(block):
    return [block] + [fetch(block, step, 0) for step in PLACES[1:]]


def spread_x(parts):
    return [parts[0]] + [fetch(parts[step], -step, 0) for step in (2, 1, 3)]


def spread_z(parts):
    return [parts[0]] + [fetch(parts[step], 0, -step) for step in (2, 1, 3)]


def exchange_row(value):
    return lax.all_to_all(value, "row", 0, 0)


def in_hbm(value):
    return pltpu.with_memory_space_constraint(value, pltpu.HBM)


def flat(value):
    return value.reshape((-1,) + value.shape[2:])


def split(value, count):
    return value.reshape((count, -1) + value.shape[1:])


def per_device(inputs, teacher, gate_weight, up_weight, down_weight, block_mask):
    tokens, width = inputs.shape
    token_count = tokens * CHIPS * CORES
    units = gate_weight.shape[1]
    half = tokens * CHIPS
    scale = float(token_count) ** 0.5
    mask = jnp.transpose(block_mask, (0, 2, 1))
    slab = shaped((Z * tokens, width))
    piece = shaped((tokens, width))
    wide, tall = shaped((width, units)), shaped((units, width))
    gates, ups, masks = ((value, other_core(value)) for value in (gate_weight, up_weight, mask))
    places = (0, 2, 1, 3)
    near = joined(gather_z(inputs, places), places, (gates[1], ups[1]))
    down = call(keep_down_kernel, tall, mask, down_weight, in_specs=[SMEM, VMEM], after=(near,))
    downs = (down, other_core(down))
    *gate_ups, partial, rows = call(
        gate_up_kernel,
        (wide,) * 4 + (shaped((half, 4 * units)), shaped((half, width))),
        *masks,
        *gather_x(near),
        in_hbm(gates[0]),
        gates[1],
        in_hbm(ups[0]),
        ups[1],
        in_specs=[SMEM] * 2 + [VMEM] * X + [ANY, VMEM] * 2,
        scratch_shapes=[pltpu.VMEM((2,) + wide.shape, wide.dtype), pltpu.SemaphoreType.DMA((2,))],
        flops=8 * half * width * units,
        vmem=16,
        after=downs[1:],
    )
    both, copies = call(
        hidden_kernel,
        (shaped((half // ROWS, 4 * units), jnp.float32), shaped((ROWS, half // ROWS, 2 * units))),
        exchange_row(split(partial, ROWS)),
    )
    hidden = flat(exchange_row(copies))
    slabs = spread_x(multiply(output_kernel, (slab,) * X, [hidden], downs))
    parts = call(sum_kernel, (piece,) * Z, *slabs)
    parts = spread_z(parts)
    student, grad_out = call(functools.partial(error_kernel, scale), (piece, piece), teacher, *parts)
    rows, hidden = hold((rows, hidden), (grad_out,))
    rows_other, hidden_other = other_core(rows), other_core(hidden)
    slabs = gather_x(joined(gather_z(grad_out)))
    partial, grad_rows = multiply(
        grad_hidden_kernel, (shaped((half, 2 * units + BLK)), shaped((half, width))), slabs, downs, (), (rows_other, hidden_other)
    )
    copies, squares = call(
        acts_kernel,
        (shaped((ROWS, half // ROWS, 4 * units)), DONE),
        exchange_row(split(partial, ROWS)),
        both,
    )
    acts = flat(exchange_row(copies))
    slabs = spread_x(multiply(grad_in_kernel, (slab,) * X, [acts], gate_ups))
    grad_rows_other, acts_other, squares_other = (other_core(value) for value in (grad_rows, acts, squares))
    grad_gate, grad_up, grad_down, loss, done = call(
        weights_kernel,
        (wide, wide, tall, shaped((1, 1), jnp.float32), DONE),
        mask,
        rows,
        rows_other,
        acts,
        acts_other,
        hidden,
        hidden_other,
        grad_rows,
        grad_rows_other,
        squares,
        squares_other,
        in_specs=[SMEM] + [VMEM] * 10,
        out_specs=(ANY,) * 3 + (VMEM,) * 2,
        scratch_shapes=[pltpu.VMEM(value.shape, value.dtype) for value in (wide, wide, tall)]
        + [pltpu.SemaphoreType.DMA((6,))],
        flops=6 * token_count * width * units,
        vmem=24,
    )
    parts = spread_z(call(sum_kernel, (piece,) * Z, *slabs))
    (grad_in,) = call(sum_kernel, (piece,), *parts, after=(done,))
    return student, loss[0, 0], grad_gate, grad_up, grad_down, grad_in


def solution(mesh):
    return jax.shard_map(
        per_device,
        mesh=mesh,
        in_specs=(
            P("col", "row"),
            P("col", "row"),
            P("row", "col"),
            P("row", "col"),
            P("col", "row"),
            P(None, "row", "col"),
        ),
        out_specs=(
            P("col", "row"),
            P(),
            P("row", "col"),
            P("row", "col"),
            P("col", "row"),
            P("col", "row"),
        ),
        check_vma=False,
    )
```
